32 devices in a mesh: fsdp: 8 (over y, x, core), rep: 4 (over z).
Axes of the slice: x: 2, y: 2, z: 4, core: 2. Of those that a mesh axis runs over, the one named last changes fastest.
Arguments:
- tokens_in: bfloat16 [2, 64, 256, 768], P(None, ('fsdp', 'rep')), may hold values from -6 to 6
- image_sizes: int32 [2, 64, 2], P(None, ('fsdp', 'rep')), may hold values from 1 to 17, as said below
- gain_one: bfloat16 [768], P('fsdp'), may hold values from 0.25 to 1.75
- shift_one: bfloat16 [768], P('fsdp'), may hold values from -3 to 3
- project_in: bfloat16 [768, 2304], P('fsdp'), may hold values from -0.21875 to 0.21875
- query_bias: bfloat16 [768], P('fsdp'), may hold values from -4 to 4
- value_bias: bfloat16 [768], P('fsdp'), may hold values from -4 to 4
- bias_table: bfloat16 [960, 12], P('fsdp'), may hold values from -4 to 4
- project_out: bfloat16 [768, 768], P('fsdp'), may hold values from -1.75 to 1.75
- out_bias: bfloat16 [768], P('fsdp'), may hold values from -3 to 3
- scale_one: bfloat16 [768], P('fsdp'), may hold values from 0.29882812 to 1.5
- gain_two: bfloat16 [768], P('fsdp'), may hold values from 0.25 to 1.75
- shift_two: bfloat16 [768], P('fsdp'), may hold values from -3 to 3
- expand_weight: bfloat16 [768, 3072], P('fsdp'), may hold values from -0.21875 to 0.21875
- expand_bias: bfloat16 [3072], P('fsdp'), may hold values from -4 to 4
- reduce_weight: bfloat16 [3072, 768], P('fsdp'), may hold values from -0.21875 to 0.21875
- reduce_bias: bfloat16 [768], P('fsdp'), may hold values from -3 to 3
- scale_two: bfloat16 [768], P('fsdp'), may hold values from 0.29882812 to 1.5
- cotangent: bfloat16 [2, 64, 256, 768], P(None, ('fsdp', 'rep')), may hold values from -6 to 6
Outputs:
- block_out: bfloat16 [2, 64, 256, 768], P(None, ('fsdp', 'rep'))
- input_grad: bfloat16 [2, 64, 256, 768], P(None, ('fsdp', 'rep'))
- grad_gain_one: float32 [768], P('fsdp')
- grad_shift_one: float32 [768], P('fsdp')
- grad_project_in: float32 [768, 2304], P('fsdp')
- grad_query_bias: float32 [768], P('fsdp')
- grad_value_bias: float32 [768], P('fsdp')
- grad_bias_table: float32 [960, 12], P('fsdp')
- grad_project_out: float32 [768, 768], P('fsdp')
- grad_out_bias: float32 [768], P('fsdp')
- grad_scale_one: float32 [768], P('fsdp')
- grad_gain_two: float32 [768], P('fsdp')
- grad_shift_two: float32 [768], P('fsdp')
- grad_expand_weight: float32 [768, 3072], P('fsdp')
- grad_expand_bias: float32 [3072], P('fsdp')
- grad_reduce_weight: float32 [3072, 768], P('fsdp')
- grad_reduce_bias: float32 [768], P('fsdp')
- grad_scale_two: float32 [768], P('fsdp')
The draws below stay inside these ranges and needn't reach their ends.
Inputs may be any that keep to these rules, and one draw needn't show every extreme that they name: image_sizes[m, i] holds the height (1 to 15) and the width (1 to 17) of image i of micro-batch m; its 1 + height * width tokens fill the first of its 256 slots, the class token first and then the patches row by row, the rest is padding; in every micro-batch some image is 15 by 17.
All inputs are finite; a program needn't handle non-finite values.
Results may differ from the reference program's by a relative error of at most 0.015.
Values may be sent and summed in bfloat16 or wider, within the bound.
No kernel may reach another device: no remote copies, remote signals or barrier semaphores. Data moves between devices by JAX's collectives and lax.ppermute only.
A program may use at most 192 MiB of HBM per device.

```python
import math
import jax
import jax.numpy as jnp
from jax import lax

D = 768
H = 12
HD = 64
FF = 3072
GH = 15
GW = 17
S = 256
NREL = 960
MB = 2
IMAGES = 64


def draw_image_sizes(key, part):
    key = jax.random.fold_in(key, 7)
    streams = jax.random.split(key, 5)
    height = 1 + jnp.maximum(jax.random.randint(streams[0], (MB, IMAGES), 0, GH), jax.random.randint(streams[1], (MB, IMAGES), 0, GH))
    width = 1 + jnp.maximum(jax.random.randint(streams[2], (MB, IMAGES), 0, GW), jax.random.randint(streams[3], (MB, IMAGES), 0, GW))
    largest = jax.random.randint(streams[4], (MB, 1), 0, IMAGES)
    marked = jnp.arange(IMAGES)[None, :] == largest
    height = jnp.where(marked, GH, height)
    width = jnp.where(marked, GW, width)
    return jnp.stack([height, width], axis=-1).astype(jnp.int32)


def block_levels(stream_key, shape, cuts, least, top_value):
    def one(dim, shards_of):
        heights = jax.random.uniform(jax.random.fold_in(jax.random.fold_in(stream_key, 6), dim), (shards_of,), jnp.float32, least / len(cuts), top_value / len(cuts))
        return jnp.repeat(jnp.exp(heights), shape[dim] // shards_of).reshape((-1,) + (1,) * (len(shape) - dim - 1))

    factor_of = one(*cuts[0])
    for cut in cuts[1:]:
        factor_of = factor_of * one(*cut)
    return factor_of


def scatter_about(own_key, dims, spread, most, cuts=(), dtype=jnp.bfloat16):
    level = block_levels(own_key, dims, cuts, -0.22, 0.18) if cuts else 1.0
    values = jax.random.normal(own_key, dims, jnp.float32) * spread * level
    return jnp.minimum(jnp.maximum(values, -most), most).astype(dtype)


def setup_inputs(seed: int = 0) -> dict:
    arg_keys = jax.random.split(jax.random.key(seed), 20)
    return {
        "tokens_in": scatter_about(arg_keys[0], (MB, IMAGES, S, D), 1.0, 6.0, ((1, 32),)),
        "image_sizes": draw_image_sizes(jax.random.fold_in(arg_keys[19], 71), 0),
        "gain_one": jnp.clip(1.0 + 0.15 * jax.random.normal(arg_keys[2], (D,), jnp.float32), 0.25, 1.75).astype(jnp.bfloat16),
        "shift_one": scatter_about(arg_keys[3], (D,), 0.3, 3.0, ((0, 8),)),
        "project_in": scatter_about(arg_keys[4], (D, 3 * D), D ** -0.5, 0.21875, ((0, 8),)),
        "query_bias": scatter_about(arg_keys[5], (D,), 0.5, 4.0, ((0, 8),)),
        "value_bias": scatter_about(arg_keys[6], (D,), 0.5, 4.0, ((0, 8),)),
        "bias_table": scatter_about(arg_keys[7], (NREL, H), 1.0, 4.0, ((0, 8),)),
        "project_out": scatter_about(arg_keys[8], (D, D), (D // 64) ** -0.5, 1.75, ((0, 8),)),
        "out_bias": scatter_about(arg_keys[9], (D,), 0.3, 3.0, ((0, 8),)),
        "scale_one": jnp.clip(jnp.exp(math.log(1.5) - 1.6133518 * jax.random.uniform(arg_keys[10], (D,), jnp.float32) ** block_levels(arg_keys[10], (D,), ((0, 8),), -0.2, 0.2)), 0.29882812, 1.5).astype(jnp.bfloat16),
        "gain_two": jnp.clip(1.0 + 0.15 * jax.random.normal(arg_keys[11], (D,), jnp.float32), 0.25, 1.75).astype(jnp.bfloat16),
        "shift_two": scatter_about(arg_keys[12], (D,), 0.3, 3.0, ((0, 8),)),
        "expand_weight": scatter_about(arg_keys[13], (D, FF), D ** -0.5, 0.21875, ((0, 8),)),
        "expand_bias": scatter_about(arg_keys[14], (FF,), 0.5, 4.0, ((0, 8),)),
        "reduce_weight": scatter_about(arg_keys[15], (FF, D), (FF // 4) ** -0.5, 0.21875, ((0, 8),)),
        "reduce_bias": scatter_about(arg_keys[16], (D,), 0.3, 3.0, ((0, 8),)),
        "scale_two": jnp.clip(jnp.exp(math.log(1.5) - 1.6133518 * jax.random.uniform(arg_keys[17], (D,), jnp.float32) ** block_levels(arg_keys[17], (D,), ((0, 8),), -0.2, 0.2)), 0.29882812, 1.5).astype(jnp.bfloat16),
        "cotangent": scatter_about(arg_keys[18], (MB, IMAGES, S, D), 1.0, 6.0, ((1, 32),)),
    }


@jax.custom_vjp
def low(v):
    return lax.optimization_barrier(v.astype(jnp.bfloat16)).astype(jnp.float32)

@jax.custom_vjp
def low_back(v):
    return v

def low_keep(v):
    return (low(v), None)

def low_pass(kept, grad):
    return (grad,)

def back_keep(v):
    return (v, None)

def back_low(kept, grad):
    return (low(grad),)
low.defvjp(low_keep, low_pass)
low_back.defvjp(back_keep, back_low)
epsilon = 1e-06
negative = -1000000000.0
highest = lax.Precision.HIGHEST

def normalize(values, gain, shift):
    center = values - lax.optimization_barrier(jnp.mean(values, axis=-1, keepdims=True))
    inverse = lax.rsqrt(lax.optimization_barrier(jnp.mean(center * center, axis=-1, keepdims=True)) + epsilon)
    return center * inverse * gain + shift

def relative_index(widths):
    slots = jnp.arange(S)
    offset = jnp.maximum(slots - 1, 0)[None, :]
    rows_at = offset // widths[:, None]
    cols_at = offset % widths[:, None]
    inner = (rows_at[:, :, None] - rows_at[:, None, :] + GH - 1) * (2 * GW - 1) + (cols_at[:, :, None] - cols_at[:, None, :] + GW - 1)
    first_zero = (slots == 0)[None, :, None]
    second_zero = (slots == 0)[None, None, :]
    index = jnp.where(first_zero & second_zero, NREL - 1, jnp.where(first_zero, NREL - 3, jnp.where(second_zero, NREL - 2, inner)))
    return jnp.clip(index, 0, NREL - 1).astype(jnp.int32)

def layer_group(params, tokens, sizes):
    gain_one, shift_one, project_in, query_bias, value_bias, bias_table, project_out, out_bias, scale_one, gain_two, shift_two, expand_weight, expand_bias, reduce_weight, reduce_bias, scale_two = params
    groups = tokens.shape[0]
    counts = 1 + sizes[:, 0] * sizes[:, 1]
    valid = jnp.arange(S)[None, :] < counts[:, None]
    index = relative_index(sizes[:, 1])
    normed = low(normalize(tokens, gain_one, shift_one))
    mixed = jnp.einsum('gtd,de->gte', normed, project_in, precision=highest)
    query = low(low_back((mixed[..., :D] + query_bias) * 0.125)).reshape(groups, S, H, HD)
    keys = low(low_back(mixed[..., D:2 * D])).reshape(groups, S, H, HD)
    values = low(low_back(mixed[..., 2 * D:] + value_bias)).reshape(groups, S, H, HD)
    both = valid[:, :, None] & valid[:, None, :]
    relative = jnp.where(both[:, None], jnp.moveaxis(bias_table[index], 3, 1), 0.0)
    scores = low_back(jnp.einsum('gshd,gthd->ghst', query, keys, precision=highest) + relative)
    scores = jnp.where(valid[:, None, None, :], scores, negative)
    probs = low(jax.nn.softmax(scores, axis=-1))
    heads = jnp.einsum('ghst,gthd->gshd', probs, values, precision=highest).reshape(groups, S, D)
    heads = low(low_back(heads))
    attended = low_back(jnp.einsum('gtd,de->gte', heads, project_out, precision=highest) + out_bias)
    middle = tokens + scale_one * attended
    normed_two = low(normalize(middle, gain_two, shift_two))
    hidden = low_back(jnp.einsum('gtd,de->gte', normed_two, expand_weight, precision=highest) + expand_bias)
    active = low(jax.nn.gelu(hidden, approximate=False))
    down = low_back(jnp.einsum('gte,ed->gtd', active, reduce_weight, precision=highest) + reduce_bias)
    return middle + scale_two * down

def reference(tokens_in, image_sizes, gain_one, shift_one, project_in, query_bias, value_bias, bias_table, project_out, out_bias, scale_one, gain_two, shift_two, expand_weight, expand_bias, reduce_weight, reduce_bias, scale_two, cotangent):
    params = (gain_one.astype(jnp.float32), shift_one.astype(jnp.float32), project_in.astype(jnp.float32), query_bias.astype(jnp.float32), value_bias.astype(jnp.float32), bias_table.astype(jnp.float32), project_out.astype(jnp.float32), out_bias.astype(jnp.float32), scale_one.astype(jnp.float32), gain_two.astype(jnp.float32), shift_two.astype(jnp.float32), expand_weight.astype(jnp.float32), expand_bias.astype(jnp.float32), reduce_weight.astype(jnp.float32), reduce_bias.astype(jnp.float32), scale_two.astype(jnp.float32))
    group = 16
    groups_count = MB * IMAGES // group
    inputs = tokens_in.astype(jnp.float32).reshape(groups_count, group, S, D)
    sizes = image_sizes.reshape(groups_count, group, 2)
    upstream = cotangent.astype(jnp.float32).reshape(groups_count, group, S, D)
    stepper = jax.checkpoint(layer_group)

    def forward(weights, values):
        return lax.map(lambda item: stepper(weights, item[0], item[1]), (values, sizes))
    result, pullback = jax.vjp(forward, params, inputs)
    weight_grads, input_grads = pullback(upstream)
    return (result.reshape(MB, IMAGES, S, D).astype(jnp.bfloat16), input_grads.reshape(MB, IMAGES, S, D).astype(jnp.bfloat16), weight_grads[0], weight_grads[1], weight_grads[2], weight_grads[3], weight_grads[4], weight_grads[5], weight_grads[6], weight_grads[7], weight_grads[8], weight_grads[9], weight_grads[10], weight_grads[11], weight_grads[12], weight_grads[13], weight_grads[14], weight_grads[15])
```

```python
import functools

import jax
import jax.numpy as jnp
from jax import lax
from jax.experimental import pallas as pl
from jax.experimental.pallas import tpu as pltpu
from jax.sharding import PartitionSpec as P

GH = 15
GW = 17
NREL = 960
SPAN = 2 * GW - 1
AHEAD = 2
CENTER = (GH - 1) * SPAN + GW - 1
HEAD = 64
SLOTS = 256

epsilon = 1e-06
negative = -1000000000.0
inv_root_tau = 0.3989422804014327
log2_e = 1.4426950408889634
VMEM_BYTES = 60 * 1024 * 1024
FAST_GROUP = 8

bf16 = jnp.bfloat16
f32 = jnp.float32


def dot_nn(left, right):
    return lax.dot_general(left, right, (((1,), (0,)), ((), ())), preferred_element_type=f32)


def dot_nt(left, right):
    return lax.dot_general(left, right, (((1,), (1,)), ((), ())), preferred_element_type=f32)


def normal_stats(values):
    center = values - jnp.mean(values, axis=-1, keepdims=True)
    inverse = lax.rsqrt(jnp.mean(center * center, axis=-1, keepdims=True) + epsilon)
    return center * inverse, inverse


def params(*semantics):
    return pltpu.CompilerParams(
        dimension_semantics=semantics, vmem_limit_bytes=VMEM_BYTES
    )


def cost(flops, nbytes):
    return pl.CostEstimate(flops=int(flops), bytes_accessed=int(nbytes), transcendentals=0)


def whole(shape):
    return pl.BlockSpec(shape, lambda *_: (0,) * len(shape))


any_spec = pl.BlockSpec(memory_space=pl.ANY)


def piece_copies(pieces, offsets, target, sems, base=0):
    return [
        pltpu.make_async_copy(
            piece,
            target.at[pl.ds(pl.multiple_of(offsets[base + k], 16), piece.shape[0])],
            sems.at[k],
        )
        for k, piece in enumerate(pieces)
    ]


VEC = dict(
    gain_one=0,
    shift_one=1,
    query_bias=2,
    value_bias=3,
    out_bias=4,
    scale_one=5,
    gain_two=6,
    shift_two=7,
    reduce_bias=8,
    scale_two=9,
)


def row(vec_ref, name):
    k = VEC[name]
    return vec_ref[k : k + 1, :]


def prepare_body(x_ref, g_ref, vec_ref, act_ref, act_t_ref, down_t_ref, sum_ref):
    step = pl.program_id(0)
    unit, _ = normal_stats(x_ref[...].astype(f32))
    act = unit * row(vec_ref, "gain_one") + row(vec_ref, "shift_one")
    act_ref[...] = act.astype(bf16)
    act_t_ref[...] = act.astype(bf16).T
    d_down = (row(vec_ref, "scale_two") * g_ref[...].astype(f32)).astype(bf16)
    down_t_ref[...] = d_down.T

    @pl.when(step == 0)
    def _():
        sum_ref[...] = jnp.zeros_like(sum_ref)

    sum_ref[...] += jnp.sum(d_down.astype(f32), axis=0, keepdims=True)


def prepare(x, g, vecs):
    tokens, width = x.shape
    block = pl.BlockSpec((SLOTS, width), lambda i: (i, 0))
    block_t = pl.BlockSpec((width, SLOTS), lambda i: (0, i))
    return pl.pallas_call(
        prepare_body,
        grid=(tokens // SLOTS,),
        in_specs=[block, block, whole(vecs.shape)],
        out_specs=[block, block_t, block_t, whole((1, width))],
        out_shape=[
            jax.ShapeDtypeStruct((tokens, width), bf16),
            jax.ShapeDtypeStruct((width, tokens), bf16),
            jax.ShapeDtypeStruct((width, tokens), bf16),
            jax.ShapeDtypeStruct((1, width), f32),
        ],
        compiler_params=params("arbitrary"),
        cost_estimate=cost(40 * tokens * width, 10 * tokens * width),
        name="prepare",
    )(x, g, vecs)


def spread(first, flip):
    spots = lax.broadcasted_iota(jnp.int32, (SLOTS, 2 * SLOTS), 0) - 1
    lanes = lax.broadcasted_iota(jnp.int32, (SLOTS, 2 * SLOTS), 1)
    target = spots + (SPAN - GW) * ((spots * 241) >> 12)
    target = jnp.where(spots >= 0, target, -1)
    if flip:
        target = jnp.where(spots >= 0, 2 * SLOTS - 1 - target, -1)
    return (lanes == target).astype(f32).astype(bf16)


def border(shape):
    q_zero = lax.broadcasted_iota(jnp.int32, shape, 0) == 0
    p_zero = lax.broadcasted_iota(jnp.int32, shape, 1) == 0
    return q_zero, p_zero


def tiles_body(flat_ref, tile_ref, place):
    @pl.when(pl.program_id(0) == 0)
    def _():
        place[...] = spread(0, False)

    flat = flat_ref[0]
    wide = jnp.broadcast_to(flat, (2 * SLOTS, 4 * SLOTS))
    shifted = pltpu.roll(wide, 4 * SLOTS - CENTER - AHEAD, 1, stride=1, stride_axis=0)
    toeplitz = shifted[:, : 2 * SLOTS].astype(bf16)
    rows_at = dot_nn(place[...], toeplitz).astype(bf16)
    inner = dot_nt(rows_at, place[...])
    q_zero, p_zero = border(inner.shape)
    last = NREL - 1 + AHEAD
    edge = jnp.where(
        p_zero,
        jnp.where(q_zero, flat[:, last : last + 1], flat[:, last - 2 : last - 1]),
        flat[:, last - 1 : last],
    )
    tile_ref[0] = jnp.where(q_zero | p_zero, edge, inner).astype(bf16)


def build_tiles(flat):
    heads = flat.shape[0]
    return pl.pallas_call(
        tiles_body,
        grid=(heads,),
        in_specs=[pl.BlockSpec((1, 1, 4 * SLOTS), lambda h: (h, 0, 0))],
        out_specs=pl.BlockSpec((1, SLOTS, SLOTS), lambda h: (h, 0, 0)),
        out_shape=jax.ShapeDtypeStruct((heads, SLOTS, SLOTS), bf16),
        scratch_shapes=[pltpu.VMEM((SLOTS, 2 * SLOTS), bf16)],
        compiler_params=params("arbitrary"),
        cost_estimate=cost(heads * 12 * SLOTS**3, heads * 4 * SLOTS**2),
        name="build_tiles",
    )(flat)


def table_body(tile_ref, flat_ref, place, flipped):
    @pl.when(pl.program_id(0) == 0)
    def _():
        place[...] = spread(0, False)
        flipped[...] = spread(0, True)

    tile = tile_ref[0]
    q_zero, p_zero = border(tile.shape)
    inner = jnp.where(q_zero | p_zero, 0.0, tile).astype(bf16)
    columns_at = dot_nn(inner, place[...]).astype(bf16)
    spread_all = lax.dot_general(
        flipped[...], columns_at, (((0,), (0,)), ((), ())), preferred_element_type=f32
    )
    wide = jnp.concatenate([spread_all, jnp.zeros_like(spread_all)], axis=1)
    shift = CENTER - (2 * SLOTS - 1) + 1
    shifted = pltpu.roll(wide, shift % (4 * SLOTS), 1, stride=1, stride_axis=0)
    flat = jnp.sum(shifted, axis=0, keepdims=True)
    lanes = lax.broadcasted_iota(jnp.int32, flat.shape, 1)
    both = jnp.sum(jnp.where(q_zero & p_zero, tile, 0.0))
    query_only = jnp.sum(jnp.where(p_zero & ~q_zero, tile, 0.0))
    key_only = jnp.sum(jnp.where(q_zero & ~p_zero, tile, 0.0))
    flat = jnp.where(lanes == NREL, both, flat)
    flat = jnp.where(lanes == NREL - 2, query_only, flat)
    flat = jnp.where(lanes == NREL - 1, key_only, flat)
    flat_ref[0] = flat


def table_grad(tiles):
    heads = tiles.shape[0]
    return pl.pallas_call(
        table_body,
        grid=(heads,),
        in_specs=[pl.BlockSpec((1, SLOTS, SLOTS), lambda h: (h, 0, 0))],
        out_specs=pl.BlockSpec((1, 1, 4 * SLOTS), lambda h: (h, 0, 0)),
        out_shape=jax.ShapeDtypeStruct((heads, 1, 4 * SLOTS), f32),
        scratch_shapes=[pltpu.VMEM((SLOTS, 2 * SLOTS), bf16)] * 2,
        compiler_params=params("arbitrary"),
        cost_estimate=cost(heads * 12 * SLOTS**3, heads * 4 * SLOTS**2),
        name="table_grad",
    )(tiles)


def place_pair(spot_row, spot_column):
    shape = (SLOTS, SLOTS)
    by_slot = lax.broadcasted_iota(jnp.int32, shape, 1) == spot_column
    by_spot = lax.broadcasted_iota(jnp.int32, shape, 0) == spot_row
    return by_slot.astype(f32).astype(bf16), by_spot.astype(f32).astype(bf16)


def in_pair(block, head):
    rest = jnp.zeros_like(block)
    return jnp.concatenate([block, rest] if head % 2 == 0 else [rest, block], axis=0)


def attend_body(
    n_pieces,
    offsets,
    act_ref,
    vec_ref,
    row_ref,
    column_ref,
    tile_ref,
    *rest,
):
    pieces = rest[:n_pieces]
    value_ref, q_t_ref, k_t_ref, exp_ref, inv_ref, heads_t_ref, heads_ref, weight, sems = rest[
        n_pieces:
    ]
    width = act_ref.shape[1]

    @pl.when(pl.program_id(0) == 0)
    def _():
        copies = piece_copies(pieces, offsets, weight, sems)
        for copy in copies:
            copy.start()
        for copy in copies:
            copy.wait()

    act = act_ref[...]
    query = (dot_nn(act, weight[:, :width]) + row(vec_ref, "query_bias")) * 0.125
    q_t = query.astype(bf16).T
    keys = dot_nn(act, weight[:, width : 2 * width]).astype(bf16)
    k_t_ref[...] = keys.T
    q_t_ref[...] = q_t
    values = dot_nn(act, weight[:, 2 * width :]) + row(vec_ref, "value_bias")
    values = values.astype(bf16)
    value_ref[...] = values
    v_t = values.T
    by_slot, by_spot = place_pair(row_ref[0], column_ref[0])
    mask = jnp.where(column_ref[0] >= 0, 0.0, negative)
    mask = jnp.broadcast_to(mask, (SLOTS, SLOTS))
    heads_count = width // HEAD
    ones = jnp.ones((16, SLOTS), bf16)
    for head in range(heads_count):
        low, high = head * HEAD, (head + 1) * HEAD
        pair = slice(head // 2 * 2 * HEAD, (head // 2 + 1) * 2 * HEAD)
        right = dot_nn(tile_ref[head], by_spot).astype(bf16)
        left_all = jnp.concatenate([by_slot, keys[:, pair]], axis=1)
        right_all = jnp.concatenate([right, in_pair(q_t[low:high], head)], axis=0)
        scores = dot_nn(left_all, right_all) + mask
        peak = jnp.max(scores, axis=0, keepdims=True)
        exponent = jnp.exp(scores - peak).astype(bf16)
        exp_ref[0, head] = exponent
        summed = dot_nn(jnp.concatenate([v_t[low:high], ones], axis=0), exponent)
        inverse = 1.0 / summed[HEAD : HEAD + 1]
        inv_ref[0, head : head + 1, :] = inverse
        heads_t_ref[low:high, :] = (summed[:HEAD] * inverse).astype(bf16)
    heads_ref[...] = heads_t_ref[...].T


def attend(offsets, act, vecs, spots, tiles, pieces):
    tokens, width = act.shape
    images = tokens // SLOTS
    heads = width // HEAD
    block = pl.BlockSpec((SLOTS, width), lambda i, _: (i, 0))
    block_t = pl.BlockSpec((width, SLOTS), lambda i, _: (0, i))
    return pl.pallas_call(
        functools.partial(attend_body, len(pieces)),
        grid_spec=pltpu.PrefetchScalarGridSpec(
            num_scalar_prefetch=1,
            grid=(images,),
            in_specs=[
                block,
                whole(vecs.shape),
                pl.BlockSpec((1, 1, SLOTS), lambda i, _: (i, 0, 0)),
                pl.BlockSpec((1, SLOTS, 1), lambda i, _: (i, 0, 0)),
                whole(tiles.shape),
            ]
            + [any_spec] * len(pieces),
            out_specs=[
                block,
                block_t,
                block_t,
                pl.BlockSpec((1, heads, SLOTS, SLOTS), lambda i, _: (i, 0, 0, 0)),
                pl.BlockSpec((1, heads, SLOTS), lambda i, _: (i, 0, 0)),
                block_t,
                block,
            ],
            scratch_shapes=[
                pltpu.VMEM((width, 3 * width), bf16),
                pltpu.SemaphoreType.DMA((len(pieces),)),
            ],
        ),
        out_shape=[
            jax.ShapeDtypeStruct((tokens, width), bf16),
            jax.ShapeDtypeStruct((width, tokens), bf16),
            jax.ShapeDtypeStruct((width, tokens), bf16),
            jax.ShapeDtypeStruct((images, heads, SLOTS, SLOTS), bf16),
            jax.ShapeDtypeStruct((images, heads, SLOTS), f32),
            jax.ShapeDtypeStruct((width, tokens), bf16),
            jax.ShapeDtypeStruct((tokens, width), bf16),
        ],
        compiler_params=params("arbitrary"),
        cost_estimate=cost(6 * tokens * width * width * 1.6, 14 * tokens * width),
        name="attend",
    )(offsets, act, vecs, spots[:, None, :], spots[:, :, None], tiles, *pieces)


def project_body(n_pieces, offsets, heads_ref, x_ref, vec_ref, *rest):
    pieces = rest[:n_pieces]
    attended_ref, middle_ref, act_ref, act_t_ref, weight, sems = rest[n_pieces:]

    @pl.when(pl.program_id(0) == 0)
    def _():
        copies = piece_copies(pieces, offsets, weight, sems)
        for copy in copies:
            copy.start()
        for copy in copies:
            copy.wait()

    attended = dot_nn(heads_ref[...], weight[...]) + row(vec_ref, "out_bias")
    attended_ref[...] = attended
    middle = x_ref[...].astype(f32) + row(vec_ref, "scale_one") * attended
    middle_ref[...] = middle
    unit, _ = normal_stats(middle)
    act = (unit * row(vec_ref, "gain_two") + row(vec_ref, "shift_two")).astype(bf16)
    act_ref[...] = act
    act_t_ref[...] = act.T


def project(offsets, heads, x, vecs, pieces):
    tokens, width = x.shape
    block = pl.BlockSpec((SLOTS, width), lambda i, _: (i, 0))
    block_t = pl.BlockSpec((width, SLOTS), lambda i, _: (0, i))
    return pl.pallas_call(
        functools.partial(project_body, len(pieces)),
        grid_spec=pltpu.PrefetchScalarGridSpec(
            num_scalar_prefetch=1,
            grid=(tokens // SLOTS,),
            in_specs=[block, block, whole(vecs.shape)] + [any_spec] * len(pieces),
            out_specs=[block, block, block, block_t],
            scratch_shapes=[
                pltpu.VMEM((width, width), bf16),
                pltpu.SemaphoreType.DMA((len(pieces),)),
            ],
        ),
        out_shape=[
            jax.ShapeDtypeStruct((tokens, width), f32),
            jax.ShapeDtypeStruct((tokens, width), f32),
            jax.ShapeDtypeStruct((tokens, width), bf16),
            jax.ShapeDtypeStruct((width, tokens), bf16),
        ],
        compiler_params=params("arbitrary"),
        cost_estimate=cost(2 * tokens * width * width, 16 * tokens * width),
        name="project",
    )(offsets, heads, x, vecs, *pieces)


def gelu_pair(hidden):
    bell = jnp.exp2(hidden * hidden * (-0.5 * log2_e))
    t = 1.0 / (1.0 + jnp.abs(hidden) * (0.3275911 * 0.7071067811865476))
    poly = 0.5 * 1.061405429
    poly = poly * t - 0.5 * 1.453152027
    poly = poly * t + 0.5 * 1.421413741
    poly = poly * t - 0.5 * 0.284496736
    poly = poly * t + 0.5 * 0.254829592
    tail = poly * t * bell
    phi = jnp.where(hidden >= 0.0, 1.0 - tail, tail)
    return hidden * phi, phi + hidden * bell * inv_root_tau


FF_BLOCK = 512


def expand_body(n_pieces, offsets, act_ref, bias_ref, *rest):
    pieces = rest[:n_pieces]
    active_ref, slope_ref, weight, sems = rest[n_pieces:]
    step = pl.program_id(0)

    @pl.when(step == 0)
    def _():
        copies = piece_copies(pieces, offsets, weight, sems)
        for copy in copies:
            copy.start()
        for copy in copies:
            copy.wait()

    start = pl.multiple_of(step * FF_BLOCK, FF_BLOCK)
    part = weight[:, pl.ds(start, FF_BLOCK)]
    for base in range(0, act_ref.shape[0], SLOTS):
        rows = slice(base, base + SLOTS)
        hidden = dot_nn(act_ref[rows, :], part) + bias_ref[...]
        active, slope = gelu_pair(hidden)
        active_ref[rows, :] = active.astype(bf16)
        slope_ref[rows, :] = slope.astype(bf16)


def expand(offsets, act, bias, pieces):
    tokens, width = act.shape
    hidden = bias.shape[1]
    block = pl.BlockSpec((tokens, FF_BLOCK), lambda i, _: (0, i))
    return pl.pallas_call(
        functools.partial(expand_body, len(pieces)),
        grid_spec=pltpu.PrefetchScalarGridSpec(
            num_scalar_prefetch=1,
            grid=(hidden // FF_BLOCK,),
            in_specs=[whole(act.shape), pl.BlockSpec((1, FF_BLOCK), lambda i, _: (0, i))]
            + [any_spec] * len(pieces),
            out_specs=[block, block],
            scratch_shapes=[
                pltpu.VMEM((width, hidden), bf16),
                pltpu.SemaphoreType.DMA((len(pieces),)),
            ],
        ),
        out_shape=[jax.ShapeDtypeStruct((tokens, hidden), bf16)] * 2,
        compiler_params=params("arbitrary"),
        cost_estimate=cost(2 * tokens * width * hidden * 1.5, 4 * tokens * hidden),
        name="expand",
    )(offsets, act, bias, *pieces)


def reduce_body(
    counts,
    offsets,
    active_ref,
    slope_ref,
    g_ref,
    middle_ref,
    attended_ref,
    vec_ref,
    *rest,
):
    n_reduce, n_expand, n_out = counts
    n_all = n_reduce + n_expand + n_out
    pieces = rest[:n_all]
    (
        out_ref,
        d_hidden_ref,
        d_middle_ref,
        d_att_ref,
        d_heads_t_ref,
        hidden_sum_ref,
        sum_ref,
        weight_r,
        weight_e,
        weight_o,
        sems,
    ) = rest[n_all:]
    step = pl.program_id(0)

    def copies_of(which):
        if which == 0:
            return piece_copies(pieces[:n_reduce], offsets, weight_r, sems.at[0], 0)
        if which == 1:
            mine = pieces[n_reduce : n_reduce + n_expand]
            return piece_copies(mine, offsets, weight_e, sems.at[1], n_reduce)
        return piece_copies(
            pieces[n_reduce + n_expand :], offsets, weight_o, sems.at[2], n_reduce + n_expand
        )

    @pl.when(step == 0)
    def _():
        for which in range(3):
            for copy in copies_of(which):
                copy.start()
        hidden_sum_ref[...] = jnp.zeros_like(hidden_sum_ref)
        sum_ref[...] = jnp.zeros_like(sum_ref)
        for copy in copies_of(0):
            copy.wait()

    g = g_ref[...].astype(f32)
    d_down = (row(vec_ref, "scale_two") * g).astype(bf16)
    d_active = dot_nt(d_down, weight_r[...])
    d_hidden = (d_active * slope_ref[...].astype(f32)).astype(bf16)
    d_hidden_ref[...] = d_hidden
    hidden_sum_ref[...] += jnp.sum(d_hidden.astype(f32), axis=0, keepdims=True)
    down = dot_nn(active_ref[...], weight_r[...]) + row(vec_ref, "reduce_bias")
    middle = middle_ref[...]
    out_ref[...] = (middle + row(vec_ref, "scale_two") * down).astype(bf16)

    @pl.when(step == 0)
    def _():
        for which in (1, 2):
            for copy in copies_of(which):
                copy.wait()

    d_act = dot_nt(d_hidden, weight_e[...])
    unit, inverse = normal_stats(middle)
    scaled = d_act * row(vec_ref, "gain_two")
    d_middle = g + inverse * (
        scaled
        - jnp.mean(scaled, axis=-1, keepdims=True)
        - unit * jnp.mean(scaled * unit, axis=-1, keepdims=True)
    )
    d_middle_ref[...] = d_middle
    d_att = (row(vec_ref, "scale_one") * d_middle).astype(bf16)
    d_att_ref[...] = d_att
    d_heads_t_ref[...] = dot_nt(weight_o[...], d_att).astype(bf16)

    def column(values):
        return jnp.sum(values, axis=0, keepdims=True)

    sum_ref[0:1] += column(g * down)
    sum_ref[1:2] += column(d_act * unit)
    sum_ref[2:3] += column(d_act)
    sum_ref[3:4] += column(d_middle * attended_ref[...])
    sum_ref[4:5] += column(d_att.astype(f32))


def reduce_back(offsets, active, slope, g, middle, attended, vecs, reduce_p, expand_p, out_p):
    tokens, hidden = active.shape
    width = g.shape[1]
    counts = (len(reduce_p), len(expand_p), len(out_p))
    block = pl.BlockSpec((SLOTS, width), lambda i, _: (i, 0))
    block_t = pl.BlockSpec((width, SLOTS), lambda i, _: (0, i))
    block_f = pl.BlockSpec((SLOTS, hidden), lambda i, _: (i, 0))
    return pl.pallas_call(
        functools.partial(reduce_body, counts),
        grid_spec=pltpu.PrefetchScalarGridSpec(
            num_scalar_prefetch=1,
            grid=(tokens // SLOTS,),
            in_specs=[block_f, block_f, block, block, block, whole(vecs.shape)]
            + [any_spec] * sum(counts),
            out_specs=[
                block,
                block_f,
                block,
                block,
                block_t,
                whole((1, hidden)),
                whole((8, width)),
            ],
            scratch_shapes=[
                pltpu.VMEM((hidden, width), bf16),
                pltpu.VMEM((width, hidden), bf16),
                pltpu.VMEM((width, width), bf16),
                pltpu.SemaphoreType.DMA((3, max(counts))),
            ],
        ),
        out_shape=[
            jax.ShapeDtypeStruct((tokens, width), bf16),
            jax.ShapeDtypeStruct((tokens, hidden), bf16),
            jax.ShapeDtypeStruct((tokens, width), f32),
            jax.ShapeDtypeStruct((tokens, width), bf16),
            jax.ShapeDtypeStruct((width, tokens), bf16),
            jax.ShapeDtypeStruct((1, hidden), f32),
            jax.ShapeDtypeStruct((8, width), f32),
        ],
        compiler_params=params("arbitrary"),
        cost_estimate=cost(
            6 * tokens * width * hidden + 2 * tokens * width * width, 7 * tokens * hidden
        ),
        name="reduce_back",
    )(offsets, active, slope, g, middle, attended, vecs, *reduce_p, *expand_p, *out_p)


def attend_back_body(
    first,
    count,
    d_heads_t_ref,
    value_ref,
    q_t_ref,
    k_t_ref,
    exp_ref,
    inv_ref,
    row_ref,
    column_ref,
    d_mixed_ref,
    tile_ref,
):
    @pl.when(pl.program_id(0) == 0)
    def _():
        tile_ref[...] = jnp.zeros_like(tile_ref)

    by_slot, by_spot = place_pair(row_ref[0], column_ref[0])
    for k in range(count):
        head = first + k
        low, high = k * HEAD, (k + 1) * HEAD
        pair = slice(k // 2 * 2 * HEAD, (k // 2 + 1) * 2 * HEAD)
        inverse = inv_ref[0, head : head + 1, :]
        exponent = exp_ref[0, k]
        wide = exponent.astype(f32)
        d_out = d_heads_t_ref[low:high, :]
        d_probs = dot_nn(value_ref[:, pair], in_pair(d_out, k))
        inner = jnp.sum(d_probs * wide, axis=0, keepdims=True) * inverse
        d_scores = ((d_probs - inner) * inverse * wide).astype(bf16)
        d_query = dot_nn(k_t_ref[low:high, :], d_scores)
        d_mixed_ref[low:high, :] = (d_query.astype(bf16) * 0.125).astype(bf16)
        base = count * HEAD
        d_keys = dot_nt(q_t_ref[low:high, :], d_scores)
        d_mixed_ref[base + low : base + high, :] = d_keys.astype(bf16)
        d_values = dot_nt((d_out.astype(f32) * inverse).astype(bf16), exponent)
        d_mixed_ref[2 * base + low : 2 * base + high, :] = d_values.astype(bf16)
        columns_at = dot_nn(d_scores, by_slot).astype(bf16)
        tile_ref[k] += dot_nn(by_spot, columns_at)


def attend_back(first, count, d_heads_t, value, q_t, k_t, exponent, inverse, spots):
    width, tokens = d_heads_t.shape
    images = tokens // SLOTS
    heads = inverse.shape[1]
    part = count * HEAD
    at = first // count
    block_t = pl.BlockSpec((part, SLOTS), lambda i: (at, i))
    return pl.pallas_call(
        functools.partial(attend_back_body, first, count),
        grid=(images,),
        in_specs=[
            block_t,
            pl.BlockSpec((SLOTS, part), lambda i: (i, at)),
            block_t,
            block_t,
            pl.BlockSpec((1, count, SLOTS, SLOTS), lambda i: (i, at, 0, 0)),
            pl.BlockSpec((1, heads, SLOTS), lambda i: (i, 0, 0)),
            pl.BlockSpec((1, 1, SLOTS), lambda i: (i, 0, 0)),
            pl.BlockSpec((1, SLOTS, 1), lambda i: (i, 0, 0)),
        ],
        out_specs=[
            pl.BlockSpec((3 * part, SLOTS), lambda i: (0, i)),
            whole((count, SLOTS, SLOTS)),
        ],
        out_shape=[
            jax.ShapeDtypeStruct((3 * part, tokens), bf16),
            jax.ShapeDtypeStruct((count, SLOTS, SLOTS), f32),
        ],
        compiler_params=params("arbitrary"),
        cost_estimate=cost(images * count * 14 * SLOTS**3, 12 * tokens * part),
        name="attend_back",
    )(d_heads_t, value, q_t, k_t, exponent, inverse, spots[:, None, :], spots[:, :, None])


def input_body(groups, offsets, x_ref, d_middle_ref, vec_ref, *rest):
    d_mixed_refs = rest[: len(groups)]
    rest = rest[len(groups) :]
    pieces = rest[:-5]
    grad_ref, sum_ref, bias_ref, weight, sems = rest[-5:]
    step = pl.program_id(0)
    width = x_ref.shape[1]

    @pl.when(step == 0)
    def _():
        copies = piece_copies(pieces, offsets, weight, sems)
        for copy in copies:
            copy.start()
        sum_ref[...] = jnp.zeros_like(sum_ref)
        bias_ref[...] = jnp.zeros_like(bias_ref)
        for copy in copies:
            copy.wait()

    total = None
    ones = jnp.ones((16, SLOTS), bf16)
    for (first, count), ref in zip(groups, d_mixed_refs, strict=True):
        part = count * HEAD
        for k in range(3):
            at = k * width + first * HEAD
            block = ref[k * part : (k + 1) * part, :]
            term = dot_nn(weight[:, at : at + part], block)
            total = term if total is None else total + term
            if k != 1:
                line = k // 2
                bias_ref[line : line + 1, first * HEAD : first * HEAD + part] += dot_nt(
                    ones, block
                )[:1]
    d_act = total.T
    unit, inverse = normal_stats(x_ref[...].astype(f32))
    sum_ref[0:1] += jnp.sum(d_act * unit, axis=0, keepdims=True)
    sum_ref[1:2] += jnp.sum(d_act, axis=0, keepdims=True)
    scaled = d_act * row(vec_ref, "gain_one")
    grad_ref[...] = (
        d_middle_ref[...]
        + inverse
        * (
            scaled
            - jnp.mean(scaled, axis=-1, keepdims=True)
            - unit * jnp.mean(scaled * unit, axis=-1, keepdims=True)
        )
    ).astype(bf16)


def input_back(offsets, x, d_middle, vecs, groups, d_mixed, pieces):
    tokens, width = x.shape
    block = pl.BlockSpec((SLOTS, width), lambda i, _: (i, 0))
    return pl.pallas_call(
        functools.partial(input_body, groups),
        grid_spec=pltpu.PrefetchScalarGridSpec(
            num_scalar_prefetch=1,
            grid=(tokens // SLOTS,),
            in_specs=[block, block, whole(vecs.shape)]
            + [pl.BlockSpec((m.shape[0], SLOTS), lambda i, _: (0, i)) for m in d_mixed]
            + [any_spec] * len(pieces),
            out_specs=[block, whole((8, width)), whole((8, width))],
            scratch_shapes=[
                pltpu.VMEM((width, 3 * width), bf16),
                pltpu.SemaphoreType.DMA((len(pieces),)),
            ],
        ),
        out_shape=[
            jax.ShapeDtypeStruct((tokens, width), bf16),
            jax.ShapeDtypeStruct((8, width), f32),
            jax.ShapeDtypeStruct((8, width), f32),
        ],
        compiler_params=params("arbitrary"),
        cost_estimate=cost(6 * tokens * width * width, 14 * tokens * width),
        name="input_back",
    )(offsets, x, d_middle, vecs, *d_mixed, *pieces)


def columns_body(order, left_ref, right_ref, out_ref):
    out_ref[0] = dot_nn(left_ref[...], right_ref[...]).astype(bf16)


def grad_columns(order, left_t, right, shards):
    width, tokens = left_t.shape
    part = right.shape[1] // shards
    blocks = order.shape[0]
    return pl.pallas_call(
        columns_body,
        grid_spec=pltpu.PrefetchScalarGridSpec(
            num_scalar_prefetch=1,
            grid=(blocks,),
            in_specs=[
                whole(left_t.shape),
                pl.BlockSpec((tokens, part), lambda i, order: (0, order[i])),
            ],
            out_specs=pl.BlockSpec((1, width, part), lambda i, _: (i, 0, 0)),
        ),
        out_shape=jax.ShapeDtypeStruct((blocks, width, part), bf16),
        compiler_params=params("arbitrary"),
        cost_estimate=cost(2 * tokens * width * part * blocks, 2 * tokens * part * blocks),
        name="grad_columns",
    )(order, left_t, right)


def rows_body(steps, transposed, column, order, *refs):
    n = len(steps)
    lefts, rights = refs[:n], refs[n : 2 * n]
    out_ref, gathered, sems = refs[2 * n :]
    step = pl.program_id(0)
    blocks = out_ref.shape[0]
    part = out_ref.shape[1]

    @pl.when(step == 0)
    def _():
        copies = [
            pltpu.make_async_copy(
                left.at[pl.ds(pl.multiple_of(order[b] * part, 16), part)],
                gathered.at[which, pl.ds(b * part, part)],
                sems.at[which, b],
            )
            for which, left in enumerate(lefts)
            for b in range(blocks)
        ]
        for copy in copies:
            copy.start()
        for copy in copies:
            copy.wait()

    start = 0
    for which in range(n):

        @pl.when((step >= start) & (step < start + steps[which]))
        def _():
            dot = dot_nt if transposed else dot_nn
            result = dot(gathered[which], rights[which][...]).astype(bf16)
            for b in range(blocks):
                out_ref[b] = result[b * part : (b + 1) * part]

        start += steps[which]


def grad_rows(order, lefts, rights, shards, column, transposed):
    width, tokens = lefts[0].shape
    part = width // shards
    blocks = order.shape[0]
    side = 0 if transposed else 1
    steps = [right.shape[side] // column for right in rights]
    in_specs = [any_spec] * len(lefts)
    start = 0
    for right, many in zip(rights, steps, strict=True):

        def index(i, _, start=start, many=many):
            at = jnp.clip(i - start, 0, many - 1)
            return (at, 0) if transposed else (0, at)

        in_specs.append(pl.BlockSpec((column, tokens) if transposed else (tokens, column), index))
        start += many
    return pl.pallas_call(
        functools.partial(rows_body, steps, transposed, column),
        grid_spec=pltpu.PrefetchScalarGridSpec(
            num_scalar_prefetch=1,
            grid=(start,),
            in_specs=in_specs,
            out_specs=pl.BlockSpec((blocks, part, column), lambda i, _: (0, 0, i)),
            scratch_shapes=[
                pltpu.VMEM((len(lefts), blocks * part, tokens), bf16),
                pltpu.SemaphoreType.DMA((len(lefts), blocks)),
            ],
        ),
        out_shape=jax.ShapeDtypeStruct((blocks, part, start * column), bf16),
        compiler_params=params("arbitrary"),
        cost_estimate=cost(
            2 * tokens * blocks * part * start * column, 2 * tokens * start * column
        ),
        name="grad_rows",
    )(order, *lefts, *rights)


def swap(values, bit):
    return lax.ppermute(values, "fsdp", [(k, k ^ bit) for k in range(FAST_GROUP)])


def gather_pieces(shard):
    rows = shard.shape[0]
    half = rows // 2
    me = lax.axis_index("fsdp")
    x_one = swap(shard, 2)
    y_one = swap(shard, 4)
    first = swap(x_one[:half], 4)
    second = swap(y_one[half:], 2)
    pieces = [shard, x_one, y_one, first, second]
    bits = [0, 2, 4, 6, 6]
    extra = [0, 0, 0, 0, half]
    offsets = [(me ^ bit) * rows + more for bit, more in zip(bits, extra)]
    offsets += [(me ^ bit ^ 1) * rows + more for bit, more in zip(bits, extra)]
    pieces = pieces + [swap(piece, 1) for piece in pieces]
    return pieces, jnp.stack(offsets).astype(jnp.int32)


def add_all(*terms):
    total = terms[0].astype(f32)
    for term in terms[1:]:
        total = total + term.astype(f32)
    return total.astype(bf16)


def scatter_sum(keep, send):
    half = keep.shape[1] // 2
    other = swap(send, 1)
    a, b = slice(0, half), slice(half, None)
    x_send = add_all(keep[1::2, a], other[1::2, a])
    y_send = add_all(keep[2:, b], other[2:, b])
    x_got = swap(x_send, 2)
    y_got = swap(y_send, 4)
    y_next = add_all(keep[2, a], other[2, a], x_got[1])
    x_next = add_all(keep[1, b], other[1, b], y_got[1])
    y_last = swap(y_next, 4)
    x_last = swap(x_next, 2)
    top = add_all(keep[0, a], other[0, a], x_got[0], y_last)
    bottom = add_all(keep[0, b], other[0, b], y_got[0], x_last)
    return jnp.concatenate([top, bottom], axis=0)


def sum_copies(values, count):
    distance = 1
    while distance < count:
        got = lax.ppermute(values, "rep", [(k, k ^ distance) for k in range(count)])
        values = add_all(values, got) if distance * 2 < count else values.astype(f32) + got.astype(f32)
        distance *= 2
    return values


def sum_small(values, count):
    for bit in (1, 2, 4):
        values = values + swap(values, bit)
    distance = 1
    while distance < count:
        values = values + lax.ppermute(values, "rep", [(k, k ^ distance) for k in range(count)])
        distance *= 2
    return values


def slot_spots(sizes):
    heights = sizes[:, 0:1]
    widths = sizes[:, 1:2]
    slots = jnp.arange(SLOTS)[None, :]
    offset = jnp.maximum(slots - 1, 0)
    spot = 1 + offset // widths * GW + offset % widths
    spot = jnp.where(slots == 0, 0, spot)
    return jnp.where(slots < 1 + heights * widths, spot, -1).astype(jnp.int32)


HEAD_GROUPS = ((0, 8), (8, 4))


def shards(
    rep_count,
    tokens_in,
    image_sizes,
    gain_one,
    shift_one,
    project_in,
    query_bias,
    value_bias,
    bias_table,
    project_out,
    out_bias,
    scale_one,
    gain_two,
    shift_two,
    expand_weight,
    expand_bias,
    reduce_weight,
    reduce_bias,
    scale_two,
    cotangent,
):
    batches, images, slots, width = tokens_in.shape
    tokens = batches * images * slots
    heads = bias_table.shape[1]
    share = gain_one.shape[0]
    group = width // share
    fast = group == FAST_GROUP
    me = lax.axis_index("fsdp")
    x = tokens_in.reshape(tokens, width)
    g = cotangent.reshape(tokens, width)
    spots = slot_spots(image_sizes.reshape(batches * images, 2))

    vectors = [gain_one, shift_one, query_bias, value_bias, out_bias, scale_one]
    vectors += [gain_two, shift_two, reduce_bias, scale_two]
    small = jnp.concatenate(vectors + [expand_bias, bias_table.reshape(-1)])
    length = small.shape[0]
    padded = -(-length // 128) * 128
    small = jnp.pad(small, (0, padded - length)).reshape(padded // 128, 128)
    small = lax.all_gather(small, "fsdp", axis=0, tiled=False).reshape(group, padded)
    count = len(vectors)
    vecs = small[:, : count * share].reshape(group, count, share)
    vecs = jnp.transpose(vecs, (1, 0, 2)).reshape(count, width).astype(f32)
    vecs = jnp.pad(vecs, ((0, 16 - count), (0, 0)))
    expand_row = small[:, count * share : count * share + expand_bias.shape[0]]
    expand_row = expand_row.reshape(1, -1).astype(f32)
    table = small[:, length - bias_table.size : length].reshape(NREL, heads)
    flat = jnp.pad(table.astype(f32).T, ((0, 0), (AHEAD, 4 * SLOTS - NREL - AHEAD)))[:, None, :]

    if fast:
        in_pieces, in_at = gather_pieces(project_in)
        out_pieces, out_at = gather_pieces(project_out)
        expand_pieces, expand_at = gather_pieces(expand_weight)
        reduce_pieces, reduce_at = gather_pieces(reduce_weight)
    else:
        zero = jnp.zeros((1,), jnp.int32)
        in_pieces, in_at = [lax.all_gather(project_in, "fsdp", axis=0, tiled=True)], zero
        out_pieces, out_at = [lax.all_gather(project_out, "fsdp", axis=0, tiled=True)], zero
        expand_pieces, expand_at = [lax.all_gather(expand_weight, "fsdp", axis=0, tiled=True)], zero
        reduce_pieces, reduce_at = [lax.all_gather(reduce_weight, "fsdp", axis=0, tiled=True)], zero

    act_one, act_one_t, d_down_t, grad_reduce_add = prepare(x, g, vecs)
    tiles = build_tiles(flat)
    value, q_t, k_t, exponent, inverse, heads_t, heads_out = attend(
        in_at, act_one, vecs, spots, tiles, in_pieces
    )
    attended, middle, act_two, act_two_t = project(out_at, heads_out, x, vecs, out_pieces)
    active, slope = expand(expand_at, act_two, expand_row, expand_pieces)

    keep_order = jnp.stack([me ^ bit for bit in (0, 2, 4, 6)]).astype(jnp.int32)
    send_order = keep_order ^ 1

    if fast:
        reduce_send = grad_columns(send_order, d_down_t, active, group)
        reduce_keep = grad_columns(keep_order, d_down_t, active, group)
        reduce_own = scatter_sum(reduce_keep, reduce_send)

    all_at = jnp.concatenate([reduce_at, expand_at, out_at])
    block_out, d_hidden, d_middle, d_att, d_heads_t, expand_sum, sums_two = reduce_back(
        all_at, active, slope, g, middle, attended, vecs, reduce_pieces, expand_pieces, out_pieces
    )

    if fast:
        lefts, rights = [act_two_t, heads_t], [d_hidden, d_att]
        middle_send = grad_rows(send_order, lefts, rights, group, 768, False)
        middle_keep = grad_rows(keep_order, lefts, rights, group, 768, False)
        middle_own = scatter_sum(middle_keep, middle_send)

    d_mixed, tile_grads, in_own = [], [], []
    for first, many in HEAD_GROUPS:
        part, tile_part = attend_back(
            first, many, d_heads_t, value, q_t, k_t, exponent, inverse, spots
        )
        d_mixed.append(part)
        tile_grads.append(tile_part)
        if fast:
            column = part.shape[0] // 3
            send = grad_rows(send_order, [act_one_t], [part], group, column, True)
            keep = grad_rows(keep_order, [act_one_t], [part], group, column, True)
            in_own.append(scatter_sum(keep, send))

    input_grad, sums_one, sums_mixed = input_back(
        in_at, x, d_middle, vecs, HEAD_GROUPS, d_mixed, in_pieces
    )
    table_flat = table_grad(jnp.concatenate(tile_grads))[:, 0, 1 : NREL + 1].T

    vector_grads = jnp.concatenate(
        [
            sums_one[0:2],
            sums_mixed[0:2],
            sums_two[4:5],
            sums_two[3:4],
            sums_two[1:3],
            grad_reduce_add,
            sums_two[0:1],
        ]
    )
    vector_grads = jnp.transpose(vector_grads.reshape(count, group, share), (1, 0, 2))
    small_grads = jnp.concatenate(
        [
            vector_grads.reshape(group, count * share),
            expand_sum.reshape(group, -1),
            table_flat.reshape(group, -1),
        ],
        axis=1,
    )

    if fast:
        small_grads = sum_small(small_grads, rep_count)
        own = lax.dynamic_slice_in_dim(small_grads, me, 1, axis=0)[0]
        grad_reduce = sum_copies(reduce_own, rep_count).T
        middle_all = sum_copies(middle_own, rep_count)
        grad_expand = middle_all[:, : expand_weight.shape[1]]
        grad_out = middle_all[:, expand_weight.shape[1] :]
        in_all = [sum_copies(value, rep_count) for value in in_own]
        parts = []
        for k in range(3):
            for (first, many), value in zip(HEAD_GROUPS, in_all):
                parts.append(value[:, k * many * HEAD : (k + 1) * many * HEAD])
        grad_in = jnp.concatenate(parts, axis=1)
    else:

        def total(values):
            values = lax.psum_scatter(values, "fsdp", scatter_dimension=0, tiled=True)
            return lax.psum(values.astype(bf16), "rep").astype(f32)

        parts = []
        for k in range(3):
            for (first, many), value in zip(HEAD_GROUPS, d_mixed):
                parts.append(value[k * many * HEAD : (k + 1) * many * HEAD])
        own = lax.psum_scatter(small_grads, "fsdp", scatter_dimension=0, tiled=True)
        own = lax.psum(own, "rep")[0]
        grad_in = total(dot_nt(act_one_t, jnp.concatenate(parts, axis=0)))
        grad_out = total(dot_nn(heads_t, d_att))
        grad_expand = total(dot_nn(act_two_t, d_hidden))
        grad_reduce = total(dot_nn(d_down_t, active).T)

    own_vectors = [own[k * share : (k + 1) * share] for k in range(count)]
    own_expand = own[count * share : count * share + expand_bias.shape[0]]
    own_table = own[count * share + expand_bias.shape[0] :].reshape(bias_table.shape)
    shape = tokens_in.shape
    return (
        block_out.reshape(shape),
        input_grad.reshape(shape),
        own_vectors[0],
        own_vectors[1],
        grad_in,
        own_vectors[2],
        own_vectors[3],
        own_table,
        grad_out,
        own_vectors[4],
        own_vectors[5],
        own_vectors[6],
        own_vectors[7],
        grad_expand,
        own_expand,
        grad_reduce,
        own_vectors[8],
        own_vectors[9],
    )


def solution(mesh):
    by_image = P(None, ("fsdp", "rep"), None, None)
    line = P("fsdp")
    matrix = P("fsdp", None)
    return jax.shard_map(
        functools.partial(shards, mesh.shape["rep"]),
        mesh=mesh,
        in_specs=(
            by_image,
            P(None, ("fsdp", "rep"), None),
            line,
            line,
            matrix,
            line,
            line,
            matrix,
            matrix,
            line,
            line,
            line,
            line,
            matrix,
            line,
            matrix,
            line,
            line,
            by_image,
        ),
        out_specs=(
            by_image,
            by_image,
            line,
            line,
            matrix,
            line,
            line,
            matrix,
            matrix,
            line,
            line,
            line,
            line,
            matrix,
            line,
            matrix,
            line,
            line,
        ),
        check_vma=False,
    )
```

```python
import functools

import jax
import jax.numpy as jnp
from jax import lax
from jax.experimental import pallas as pl
from jax.experimental.pallas import tpu as pltpu
from jax.sharding import PartitionSpec as P

GH = 15
GW = 17
NREL = 960
SPAN = 2 * GW - 1
AHEAD = 2
CENTER = (GH - 1) * SPAN + GW - 1
HEAD = 64
SLOTS = 256

epsilon = 1e-06
negative = -1000000000.0
inv_root_two = 0.7071067811865476
inv_root_tau = 0.3989422804014327
log2_e = 1.4426950408889634
MIB = 1024 * 1024
FAST_GROUP = 8

bf16 = jnp.bfloat16
f32 = jnp.float32


def dot_nn(left, right):
    return lax.dot_general(left, right, (((1,), (0,)), ((), ())), preferred_element_type=f32)


def dot_nt(left, right):
    return lax.dot_general(left, right, (((1,), (1,)), ((), ())), preferred_element_type=f32)


def dot_tn(left, right):
    return lax.dot_general(left, right, (((0,), (0,)), ((), ())), preferred_element_type=f32)


def normal_stats(values):
    center = values - jnp.mean(values, axis=-1, keepdims=True)
    inverse = lax.rsqrt(jnp.mean(center * center, axis=-1, keepdims=True) + epsilon)
    return center * inverse, inverse


def params(mib, *semantics):
    return pltpu.CompilerParams(dimension_semantics=semantics, vmem_limit_bytes=mib * MIB)


COST = 0.25


def cost(flops, nbytes):
    return pl.CostEstimate(
        flops=int(COST * flops), bytes_accessed=int(COST * nbytes), transcendentals=0
    )


def whole(shape):
    return pl.BlockSpec(shape, lambda *_: (0,) * len(shape), pipeline_mode=pl.Buffered(1))


def near(shape, dtype):
    return pltpu.VMEM(shape, dtype)


def far(shape, dtype):
    return pltpu.HBM(shape, dtype)


TOKEN = (8, 128)


def in_vmem(value):
    return pltpu.with_memory_space_constraint(value, pltpu.VMEM)


def in_hbm(value):
    return pltpu.with_memory_space_constraint(value, pltpu.HBM)


any_spec = pl.BlockSpec(memory_space=pl.ANY)


def piece_copies(pieces, offsets, target, sems, base=0, column=0):
    width = target.shape[1]
    return [
        pltpu.make_async_copy(
            piece if piece.shape[1] == width else piece.at[:, column : column + width],
            target.at[pl.ds(pl.multiple_of(offsets[base + k], 16), piece.shape[0])],
            sems.at[k],
        )
        for k, piece in enumerate(pieces)
    ]


PACK_ROWS = 32
BIAS_ROWS = 10
TABLE_ROWS = 16


def pack_body(*refs):
    vectors, bias_ref, table_ref, out_ref, rows = refs[:-4], refs[-4], refs[-3], refs[-2], refs[-1]
    rows[...] = jnp.zeros_like(rows)
    share = vectors[0].shape[1]
    for k, ref in enumerate(vectors):
        rows[k : k + 1, 0:share] = ref[...].astype(f32)
    for k in range(bias_ref.shape[0]):
        rows[BIAS_ROWS + k : BIAS_ROWS + k + 1, 0 : bias_ref.shape[1]] = bias_ref[k : k + 1].astype(
            f32
        )
    heads, many = table_ref.shape
    rows[TABLE_ROWS : TABLE_ROWS + heads, 0:many] = table_ref[...].astype(f32)
    out_ref[...] = rows[...].astype(bf16)


def mover(wide, start, many):
    lanes = lax.broadcasted_iota(jnp.int32, (128, wide), 1)
    rows = lax.broadcasted_iota(jnp.int32, (128, wide), 0)
    return ((lanes == rows + start) & (rows < many)).astype(f32).astype(bf16)


def unpack_body(group, share, bias_share, table_share, got_ref, vec_ref, bias_ref, flat_ref):
    vectors, flats, line = None, None, None
    for k in range(group):
        first, second = got_ref[k, 0:16], got_ref[k, 16:32]
        term = dot_nn(first, mover(vec_ref.shape[1], k * share, share))
        vectors = term if vectors is None else vectors + term
        term = dot_nn(second, mover(flat_ref.shape[1], AHEAD + k * table_share, table_share))
        flats = term if flats is None else flats + term
        wide = first.astype(f32)
        for part in range(-(-bias_share // 128)):
            base = k * bias_share + part * 128
            size = min(128, bias_share - part * 128)
            if size == 128:
                bias_ref[:, base : base + 128] = wide[BIAS_ROWS + part : BIAS_ROWS + part + 1]
            else:
                term = dot_nn(first, mover(bias_ref.shape[1], base, size))
                term = term[BIAS_ROWS + part : BIAS_ROWS + part + 1]
                line = term if line is None else line + term
    vec_ref[...] = vectors
    flat_ref[...] = flats
    if line is not None:
        bias_ref[...] = line


def gather_small(vectors, bias, table, group):
    share = vectors[0].shape[0]
    packed = pl.pallas_call(
        pack_body,
        out_shape=jax.ShapeDtypeStruct((PACK_ROWS, 128), bf16),
        scratch_shapes=[pltpu.VMEM((PACK_ROWS, 128), f32)],
        name="pack",
    )(
        *[vector.reshape(1, share) for vector in vectors],
        bias.reshape(-1, min(128, bias.shape[0])),
        table.T,
    )
    got = lax.all_gather(packed, "fsdp", axis=0, tiled=False)
    unpacked = pl.pallas_call(
        functools.partial(unpack_body, group, share, bias.shape[0], table.shape[0]),
        out_shape=[
            jax.ShapeDtypeStruct((16, group * share), f32),
            jax.ShapeDtypeStruct((1, group * bias.shape[0]), f32),
            jax.ShapeDtypeStruct((16, 4 * SLOTS), f32),
        ],
        compiler_params=params(16),
        name="unpack",
    )(got)
    return *unpacked, got


def sums_body(group, share, bias_share, table_share, one_ref, mixed_ref, two_ref, down_ref, last_ref, bias_ref, flat_ref, out_ref):
    lines = jnp.concatenate(
        [
            one_ref[0:2],
            mixed_ref[0:2],
            two_ref[3:4],
            two_ref[2:3],
            two_ref[0:2],
            down_ref[...],
            last_ref[...],
            jnp.zeros((6, one_ref.shape[1]), f32),
        ],
        axis=0,
    )
    wide = lines.shape[1]
    flat = jnp.concatenate([flat_ref[...], jnp.zeros((4, flat_ref.shape[1]), f32)], axis=0)
    bias = jnp.broadcast_to(bias_ref[...], (8, bias_ref.shape[1]))
    for k in range(group):
        at = k * share
        moved = lines if at == 0 else pltpu.roll(lines, wide - at, 1)
        out_ref[k, 0:16] = moved[:, :128]
        for part in range(-(-bias_share // 128)):
            base = k * bias_share + part * 128
            moved = bias if base == 0 else pltpu.roll(bias, bias.shape[1] - base, 1)
            out_ref[k, BIAS_ROWS + part : BIAS_ROWS + part + 1] = moved[:1, :128]
        at = 1 + k * table_share
        out_ref[k, 16:32] = pltpu.roll(flat, flat.shape[1] - at, 1)[:, :128]


def pack_sums(group, share, bias_share, table_share, *sums):
    return pl.pallas_call(
        functools.partial(sums_body, group, share, bias_share, table_share),
        out_shape=jax.ShapeDtypeStruct((group, PACK_ROWS, 128), f32),
        compiler_params=params(16),
        name="pack_sums",
    )(*sums)


VEC = dict(
    gain_one=0,
    shift_one=1,
    query_bias=2,
    value_bias=3,
    out_bias=4,
    scale_one=5,
    gain_two=6,
    shift_two=7,
    reduce_bias=8,
    scale_two=9,
)


def row(vec_ref, name):
    k = VEC[name]
    return vec_ref[k : k + 1, :]


def prepare_body(x_ref, g_ref, vec_ref, act_ref, act_t_ref, down_ref, sum_ref):
    step = pl.program_id(0)
    unit, _ = normal_stats(x_ref[...].astype(f32))
    act = unit * row(vec_ref, "gain_one") + row(vec_ref, "shift_one")
    act_ref[...] = act.astype(bf16)
    act_t_ref[...] = act.astype(bf16).T
    d_down = (row(vec_ref, "scale_two") * g_ref[...].astype(f32)).astype(bf16)
    down_ref[...] = d_down

    @pl.when(step == 0)
    def _():
        sum_ref[...] = jnp.zeros_like(sum_ref)

    sum_ref[...] += jnp.sum(d_down.astype(f32), axis=0, keepdims=True)


def prepare(x, g, vecs):
    tokens, width = x.shape
    block = pl.BlockSpec((SLOTS, width), lambda i: (i, 0))
    block_t = pl.BlockSpec((width, SLOTS), lambda i: (0, i))
    return pl.pallas_call(
        prepare_body,
        grid=(tokens // SLOTS,),
        in_specs=[block, block, whole(vecs.shape)],
        out_specs=[block, block_t, block, whole((1, width))],
        out_shape=[
            near((tokens, width), bf16),
            far((width, tokens), bf16),
            near((tokens, width), bf16),
            jax.ShapeDtypeStruct((1, width), f32),
        ],
        compiler_params=params(16, "arbitrary"),
        cost_estimate=cost(40 * tokens * width, 10 * tokens * width),
        name="prepare",
    )(in_hbm(x), in_hbm(g), vecs)


def spread(flip):
    spots = lax.broadcasted_iota(jnp.int32, (SLOTS, 2 * SLOTS), 0) - 1
    lanes = lax.broadcasted_iota(jnp.int32, (SLOTS, 2 * SLOTS), 1)
    target = spots + (SPAN - GW) * ((spots * 241) >> 12)
    target = jnp.where(spots >= 0, target, -1)
    if flip:
        target = jnp.where(spots >= 0, 2 * SLOTS - 1 - target, -1)
    return (lanes == target).astype(f32).astype(bf16)


def border(shape):
    q_zero = lax.broadcasted_iota(jnp.int32, shape, 0) == 0
    p_zero = lax.broadcasted_iota(jnp.int32, shape, 1) == 0
    return q_zero, p_zero


def tiles_body(flat_ref, tile_ref, token_ref, place, toeplitz, rows_at):
    heads = tile_ref.shape[0]
    token_ref[...] = jnp.zeros_like(token_ref)
    place[...] = spread(False)
    for head in range(heads):
        flat = jnp.broadcast_to(flat_ref[head : head + 1, :], (8, 4 * SLOTS))
        base = pltpu.roll(flat, 4 * SLOTS - CENTER - AHEAD, 1, stride=1, stride_axis=0)
        for k in range(0, 16, 2):
            pair = [base if k == 0 else pltpu.roll(base, 8 * k, 1), pltpu.roll(base, 8 * k + 8, 1)]
            pair = jnp.concatenate(pair, axis=0).astype(bf16)
            for m in range(4):
                start = 4 * SLOTS - 128 * m
                both = pair
                if m:
                    both = jnp.concatenate([both[:, start:], both[:, :start]], axis=1)
                toeplitz[head, 128 * m + 8 * k : 128 * m + 8 * k + 16] = both[:, : 2 * SLOTS]
    for head in range(heads):
        rows_at[head] = dot_nn(place[...], toeplitz[head]).astype(bf16)
    q_zero, p_zero = border((SLOTS, SLOTS))
    last = NREL - 1 + AHEAD
    for head in range(heads):
        inner = dot_nt(rows_at[head], place[...])
        flat = flat_ref[head : head + 1, :]
        edge = jnp.where(
            p_zero,
            jnp.where(q_zero, flat[:, last : last + 1], flat[:, last - 2 : last - 1]),
            flat[:, last - 1 : last],
        )
        tile_ref[head] = jnp.where(q_zero | p_zero, edge, inner).astype(bf16)


def build_tiles(flat, heads):
    return pl.pallas_call(
        tiles_body,
        out_shape=[near((heads, SLOTS, SLOTS), bf16), jax.ShapeDtypeStruct(TOKEN, f32)],
        scratch_shapes=[
            pltpu.VMEM((SLOTS, 2 * SLOTS), bf16),
            pltpu.VMEM((heads, 2 * SLOTS, 2 * SLOTS), bf16),
            pltpu.VMEM((heads, SLOTS, 2 * SLOTS), bf16),
        ],
        compiler_params=params(24),
        cost_estimate=cost(heads * 12 * SLOTS**3, heads * 4 * SLOTS**2),
        name="build_tiles",
    )(flat)


def table_body(_, *refs):
    tile_refs, (flat_ref, place, flipped, inner, columns_at, spreads) = refs[:-6], refs[-6:]
    place[...] = spread(False)
    flipped[...] = spread(True).T
    q_zero, p_zero = border((SLOTS, SLOTS))
    inside = jnp.where(q_zero | p_zero, 0.0, 1.0)
    tiles = [ref.at[k] for ref in tile_refs for k in range(ref.shape[0])]
    for head, tile in enumerate(tiles):
        inner[head] = (tile[...] * inside).astype(bf16)
    for head in range(len(tiles)):
        columns_at[head] = dot_nn(inner[head], place[...]).astype(bf16)
    for head in range(len(tiles)):
        spreads[head] = dot_nn(flipped[...], columns_at[head])
    lanes = lax.broadcasted_iota(jnp.int32, (1, 4 * SLOTS), 1)
    for head, tile in enumerate(tiles):
        total = None
        for k in range(16):
            lines = None
            for m in range(4):
                at = 128 * m + 8 * k
                parts = [jnp.zeros((8, 128 * m), f32)] if m else []
                parts.append(spreads[head, at : at + 8])
                parts.append(jnp.zeros((8, 2 * SLOTS - 128 * m), f32))
                term = jnp.concatenate(parts, axis=1)
                lines = term if lines is None else lines + term
            lines = pltpu.roll(lines, (8 * k - 32) % (4 * SLOTS), 1)
            total = lines if total is None else total + lines
        total = pltpu.roll(total, 0, 1, stride=1, stride_axis=0)
        flat = jnp.sum(total, axis=0, keepdims=True)
        both = tile[0:1, 0:1]
        query_only = jnp.sum(tile[:, 0:1], axis=0, keepdims=True) - both
        key_only = jnp.sum(tile[0:1, :], axis=1, keepdims=True) - both
        flat = jnp.where(lanes == NREL, both, flat)
        flat = jnp.where(lanes == NREL - 2, query_only, flat)
        flat_ref[head : head + 1] = jnp.where(lanes == NREL - 1, key_only, flat)


def table_grad(numbers, *tiles):
    heads = sum(part.shape[0] for part in tiles)
    return pl.pallas_call(
        table_body,
        in_specs=[pl.BlockSpec(memory_space=pltpu.SMEM)]
        + [pl.BlockSpec(memory_space=pltpu.VMEM)] * len(tiles),
        out_shape=jax.ShapeDtypeStruct((heads, 4 * SLOTS), f32),
        scratch_shapes=[
            pltpu.VMEM((SLOTS, 2 * SLOTS), bf16),
            pltpu.VMEM((2 * SLOTS, SLOTS), bf16),
            pltpu.VMEM((heads, SLOTS, SLOTS), bf16),
            pltpu.VMEM((heads, SLOTS, 2 * SLOTS), bf16),
            pltpu.VMEM((heads, 2 * SLOTS, 2 * SLOTS), f32),
        ],
        compiler_params=params(32),
        cost_estimate=cost(heads * 12 * SLOTS**3, heads * 4 * SLOTS**2),
        name="table_grad",
    )(numbers, *map(in_vmem, tiles))


def spot_at(slots, sizes, image):
    count, wide, per = sizes[3 * image], sizes[3 * image + 1], sizes[3 * image + 2]
    offset = jnp.maximum(slots - 1, 0)
    line = (offset * per) >> 16
    spot = 1 + offset + line * (GW - wide)
    spot = jnp.where(slots == 0, 0, spot)
    return jnp.where(slots < count, spot, -1)


def place_pair(sizes, image):
    shape = (SLOTS, SLOTS)
    down = lax.broadcasted_iota(jnp.int32, shape, 0)
    along = lax.broadcasted_iota(jnp.int32, shape, 1)
    by_slot = spot_at(down, sizes, image) == along
    by_spot = spot_at(along, sizes, image) == down
    return by_slot.astype(f32).astype(bf16), by_spot.astype(f32).astype(bf16)


def in_pair(block, head):
    rest = jnp.zeros_like(block)
    return jnp.concatenate([block, rest] if head % 2 == 0 else [rest, block], axis=0)


CHIPS = 4
CORE = 4
KEPT = 5
SENT = 9
SIZES = 13


def attend_body(at, n_pieces, numbers, act_ref, vec_ref, tile_ref, *rest):
    pieces = rest[:n_pieces]
    value_ref, q_t_ref, k_t_ref, exp_ref, inv_ref, heads_t_ref, heads_ref = rest[n_pieces:-4]
    weight, rights, scores, sems = rest[-4:]
    width = act_ref.shape[1]
    image = pl.program_id(0)

    @pl.when(image == 0)
    def _():
        copies = piece_copies(pieces, numbers, weight, sems, at)
        for copy in copies:
            copy.start()
        for copy in copies:
            copy.wait()

    sizes = [numbers[SIZES + 3 * image + k] for k in range(3)]
    by_slot, by_spot = place_pair(sizes, 0)
    heads = width // HEAD
    act = act_ref[...]
    query = (dot_nn(act, weight[:, :width]) + row(vec_ref, "query_bias")) * 0.125
    keys = dot_nn(act, weight[:, width : 2 * width]).astype(bf16)
    values = (dot_nn(act, weight[:, 2 * width :]) + row(vec_ref, "value_bias")).astype(bf16)
    rights[...] = (
        dot_nn(tile_ref[...].reshape(heads * SLOTS, SLOTS), by_spot)
        .astype(bf16)
        .reshape(heads, SLOTS, SLOTS)
    )
    q_t_ref[...] = query.astype(bf16).T
    k_t_ref[...] = keys.T
    value_ref[...] = values
    v_t = values.T
    slots = lax.broadcasted_iota(jnp.int32, (SLOTS, SLOTS), 0)
    mask = jnp.where(slots < sizes[0], 0.0, negative)
    ones = jnp.ones((16, SLOTS), bf16)
    for head in range(heads):
        low, high = head * HEAD, (head + 1) * HEAD
        pair = slice(head // 2 * 2 * HEAD, (head // 2 + 1) * 2 * HEAD)
        left = jnp.concatenate([by_slot, keys[:, pair]], axis=1)
        right = jnp.concatenate([rights[head], in_pair(q_t_ref[low:high, :], head)], axis=0)
        scores[head] = dot_nn(left, right) + mask
    for head in range(heads):
        score = scores[head]
        peak = jnp.max(score, axis=0, keepdims=True)
        exp_ref[0, head] = jnp.exp(score - peak).astype(bf16)
    for head in range(heads):
        low, high = head * HEAD, (head + 1) * HEAD
        summed = dot_nn(jnp.concatenate([v_t[low:high], ones], axis=0), exp_ref[0, head])
        inverse = 1.0 / summed[HEAD : HEAD + 1]
        inv_ref[0, head : head + 1, :] = inverse
        heads_t_ref[low:high, :] = (summed[:HEAD] * inverse).astype(bf16)
    heads_ref[...] = heads_t_ref[...].T


def attend(at, numbers, act, vecs, tiles, pieces):
    tokens, width = act.shape
    images = tokens // SLOTS
    heads = width // HEAD
    block = pl.BlockSpec((SLOTS, width), lambda i, _: (i, 0))
    block_t = pl.BlockSpec((width, SLOTS), lambda i, _: (0, i))
    return pl.pallas_call(
        functools.partial(attend_body, at, len(pieces)),
        grid_spec=pltpu.PrefetchScalarGridSpec(
            num_scalar_prefetch=1,
            grid=(images,),
            in_specs=[block, whole(vecs.shape), whole(tiles.shape)] + [any_spec] * len(pieces),
            out_specs=[
                block,
                block_t,
                block_t,
                pl.BlockSpec((1, heads, SLOTS, SLOTS), lambda i, _: (i, 0, 0, 0)),
                pl.BlockSpec((1, heads, SLOTS), lambda i, _: (i, 0, 0)),
                block_t,
                block,
            ],
            scratch_shapes=[
                pltpu.VMEM((width, 3 * width), bf16),
                pltpu.VMEM((heads, SLOTS, SLOTS), bf16),
                pltpu.VMEM((heads, SLOTS, SLOTS), f32),
                pltpu.SemaphoreType.DMA((len(pieces),)),
            ],
        ),
        out_shape=[
            far((tokens, width), bf16),
            far((width, tokens), bf16),
            far((width, tokens), bf16),
            far((images, heads, SLOTS, SLOTS), bf16),
            far((images, heads, SLOTS), f32),
            far((width, tokens), bf16),
            near((tokens, width), bf16),
        ],
        compiler_params=params(32, "arbitrary"),
        cost_estimate=cost(6 * tokens * width * width * 1.6, 14 * tokens * width),
        name="attend",
    )(numbers, in_vmem(act), vecs, in_vmem(tiles), *map(in_hbm, pieces))


def project_body(at, n_pieces, offsets, heads_ref, x_ref, vec_ref, *rest):
    pieces = rest[:n_pieces]
    attended_ref, middle_ref, act_ref, act_t_ref, token_ref, weight, sems = rest[n_pieces:]

    @pl.when(pl.program_id(0) == 0)
    def _():
        copies = piece_copies(pieces, offsets, weight, sems, at, 3 * weight.shape[0])
        for copy in copies:
            copy.start()
        for copy in copies:
            copy.wait()

    token_ref[...] = jnp.zeros_like(token_ref)
    attended = dot_nn(heads_ref[...], weight[...]) + row(vec_ref, "out_bias")
    attended_ref[...] = attended.astype(bf16)
    middle = x_ref[...].astype(f32) + row(vec_ref, "scale_one") * attended
    middle_ref[...] = middle
    unit, _ = normal_stats(middle)
    act = (unit * row(vec_ref, "gain_two") + row(vec_ref, "shift_two")).astype(bf16)
    act_ref[...] = act
    act_t_ref[...] = act.T


def project(at, offsets, heads, x, vecs, pieces):
    tokens, width = x.shape
    block = pl.BlockSpec((SLOTS, width), lambda i, _: (i, 0))
    block_t = pl.BlockSpec((width, SLOTS), lambda i, _: (0, i))
    return pl.pallas_call(
        functools.partial(project_body, at, len(pieces)),
        grid_spec=pltpu.PrefetchScalarGridSpec(
            num_scalar_prefetch=1,
            grid=(tokens // SLOTS,),
            in_specs=[block, block, whole(vecs.shape)] + [any_spec] * len(pieces),
            out_specs=[block, block, block, block_t, whole(TOKEN)],
            scratch_shapes=[
                pltpu.VMEM((width, width), bf16),
                pltpu.SemaphoreType.DMA((len(pieces),)),
            ],
        ),
        out_shape=[
            near((tokens, width), bf16),
            near((tokens, width), f32),
            near((tokens, width), bf16),
            near((width, tokens), bf16),
            jax.ShapeDtypeStruct(TOKEN, f32),
        ],
        compiler_params=params(20, "arbitrary"),
        cost_estimate=cost(2 * tokens * width * width, 16 * tokens * width),
        name="project",
    )(offsets, in_vmem(heads), in_hbm(x), vecs, *map(in_hbm, pieces))


def expand_body(at, n_pieces, numbers, act_ref, down_ref, bias_ref, *rest):
    pieces = rest[:n_pieces]
    active_ref, slope_ref, keep_ref, send_ref, token_ref, weight, hidden_s, active_s, grad_s, sems = rest[n_pieces:]
    step = pl.program_id(0)
    part = bias_ref.shape[1]

    def copies_of(at_step):
        column = pl.multiple_of(numbers[at_step] * part, part)
        return [
            pltpu.make_async_copy(
                piece.at[:, pl.ds(column, part)],
                weight.at[
                    at_step, pl.ds(pl.multiple_of(numbers[at + k], 16), piece.shape[0])
                ],
                sems.at[at_step, k],
            )
            for k, piece in enumerate(pieces)
        ]

    @pl.when(step == 0)
    def _():
        for k in range(CHIPS):
            for copy in copies_of(k):
                copy.start()

    for copy in copies_of(step):
        copy.wait()

    token_ref[...] = jnp.zeros_like(token_ref)
    hidden_s[...] = dot_nn(act_ref[...], weight[step]) + bias_ref[...]
    hidden = hidden_s[...]
    phi = 0.5 + 0.5 * lax.erf(hidden * inv_root_two)
    active = (hidden * phi).astype(bf16)
    active_s[...] = active
    active_ref[...] = active
    bell = jnp.exp2(hidden * hidden * (-0.5 * log2_e))
    slope_ref[...] = (phi + hidden * bell * inv_root_tau).astype(bf16)
    grad_s[...] = dot_tn(active_s[...], down_ref[...]).astype(bf16)
    half = part // 2
    kept = pl.multiple_of(numbers[CORE] * half, half)
    keep_ref[0] = grad_s[pl.ds(kept, half), :]
    send_ref[0] = grad_s[pl.ds(pl.multiple_of(half - kept, half), half), :]


def expand(at, numbers, act, d_down, bias, pieces):
    tokens, width = act.shape
    hidden = bias.shape[1]
    part = hidden // CHIPS
    block = pl.BlockSpec((tokens, part), lambda i, numbers: (0, numbers[i]))
    grad = pl.BlockSpec((1, part // 2, width), lambda i, _: (i, 0, 0))
    return pl.pallas_call(
        functools.partial(expand_body, at, len(pieces)),
        grid_spec=pltpu.PrefetchScalarGridSpec(
            num_scalar_prefetch=1,
            grid=(CHIPS,),
            in_specs=[
                whole(act.shape),
                whole(d_down.shape),
                pl.BlockSpec((1, part), lambda i, numbers: (0, numbers[i])),
            ]
            + [any_spec] * len(pieces),
            out_specs=[block, block, grad, grad, whole(TOKEN)],
            scratch_shapes=[
                pltpu.VMEM((CHIPS, width, part), bf16),
                pltpu.VMEM((tokens, part), f32),
                pltpu.VMEM((tokens, part), bf16),
                pltpu.VMEM((part, width), bf16),
                pltpu.SemaphoreType.DMA((CHIPS, len(pieces))),
            ],
        ),
        out_shape=[far((tokens, hidden), bf16), near((tokens, hidden), bf16)]
        + [far((CHIPS, part // 2, width), bf16)] * 2
        + [jax.ShapeDtypeStruct(TOKEN, f32)],
        compiler_params=params(36, "arbitrary"),
        cost_estimate=cost(4 * tokens * width * hidden * 1.2, 4 * tokens * hidden),
        name="expand",
    )(numbers, in_vmem(act), in_vmem(d_down), bias, *map(in_hbm, pieces))


def hidden_body(at, n_pieces, groups, numbers, down_ref, slope_ref, left_ref, *rest):
    pieces = rest[:n_pieces]
    d_hidden_ref, sum_ref, keep_ref, send_ref, weight, gathered, d_hidden_s, sems, left_sems = rest[
        n_pieces:
    ]
    step = pl.program_id(0)
    part = slope_ref.shape[1]
    share = keep_ref.shape[1]
    lefts = [
        pltpu.make_async_copy(
            left_ref.at[pl.ds(pl.multiple_of(numbers[KEPT + b] * share, 16), share)],
            gathered.at[pl.ds(b * share, share)],
            left_sems.at[b],
        )
        for b in range(2 * CHIPS)
    ]
    copies = piece_copies(pieces, numbers, weight, sems, at)

    @pl.when(step == 0)
    def _():
        for copy in copies:
            copy.start()
        for copy in lefts:
            copy.start()

    for at_step in range(CHIPS):

        @pl.when(step == at_step)
        def _():
            for k, copy in enumerate(copies):
                if groups[k] == at_step:
                    copy.wait()

    rows = weight[pl.ds(pl.multiple_of(step * part, part), part), :]
    d_hidden = (dot_nt(down_ref[...], rows) * slope_ref[...].astype(f32)).astype(bf16)
    d_hidden_s[...] = d_hidden
    d_hidden_ref[...] = d_hidden
    sum_ref[...] = jnp.sum(d_hidden.astype(f32), axis=0, keepdims=True)

    @pl.when(step == 0)
    def _():
        for copy in lefts:
            copy.wait()

    grad = dot_nn(gathered[...], d_hidden_s[...]).astype(bf16)
    for b in range(CHIPS):
        keep_ref[b] = grad[b * share : (b + 1) * share]
        send_ref[b] = grad[(CHIPS + b) * share : (CHIPS + b + 1) * share]


def hidden_back(at, numbers, d_down, slope, act_t, pieces, groups):
    tokens, hidden = slope.shape
    width = d_down.shape[1]
    part = hidden // CHIPS
    share = width // (2 * CHIPS)
    block = pl.BlockSpec((tokens, part), lambda i, numbers: (0, numbers[i]))
    grad = pl.BlockSpec((CHIPS, share, part), lambda i, numbers: (0, 0, numbers[i]))
    return pl.pallas_call(
        functools.partial(hidden_body, at, len(pieces), groups),
        grid_spec=pltpu.PrefetchScalarGridSpec(
            num_scalar_prefetch=1,
            grid=(CHIPS,),
            in_specs=[whole(d_down.shape), block, any_spec] + [any_spec] * len(pieces),
            out_specs=[
                block,
                pl.BlockSpec((1, part), lambda i, numbers: (0, numbers[i])),
                grad,
                grad,
            ],
            scratch_shapes=[
                pltpu.VMEM((hidden, width), bf16),
                pltpu.VMEM((width, tokens), bf16),
                pltpu.VMEM((tokens, part), bf16),
                pltpu.SemaphoreType.DMA((len(pieces),)),
                pltpu.SemaphoreType.DMA((2 * CHIPS,)),
            ],
        ),
        out_shape=[
            near((tokens, hidden), bf16),
            jax.ShapeDtypeStruct((1, hidden), f32),
            far((CHIPS, share, hidden), bf16),
            far((CHIPS, share, hidden), bf16),
        ],
        compiler_params=params(36, "arbitrary"),
        cost_estimate=cost(4 * tokens * width * hidden * 1.1, 4 * tokens * hidden),
        name="hidden_back",
    )(numbers, in_vmem(d_down), in_vmem(slope), in_vmem(act_t), *map(in_hbm, pieces))


def norm_body(at, counts, numbers, d_hidden_ref, g_ref, middle_ref, attended_ref, vec_ref, *rest):
    n_expand, n_out = counts
    pieces = rest[: n_expand + n_out]
    d_middle_ref, d_att_ref, d_heads_t_ref, sum_ref, weight_e, weight_o, sems = rest[
        n_expand + n_out :
    ]
    step = pl.program_id(0)
    first = piece_copies(pieces[:n_expand], numbers, weight_e, sems.at[0], at[0])
    second = piece_copies(
        pieces[n_expand:], numbers, weight_o, sems.at[1], at[1], 3 * weight_o.shape[0]
    )

    @pl.when(step == 0)
    def _():
        for copy in first + second:
            copy.start()
        sum_ref[...] = jnp.zeros_like(sum_ref)
        for copy in first + second:
            copy.wait()

    middle = middle_ref[...]
    unit, inverse = normal_stats(middle)
    d_act = dot_nt(d_hidden_ref[...], weight_e[...])
    scaled = d_act * row(vec_ref, "gain_two")
    d_middle = g_ref[...].astype(f32) + inverse * (
        scaled
        - jnp.mean(scaled, axis=-1, keepdims=True)
        - unit * jnp.mean(scaled * unit, axis=-1, keepdims=True)
    )
    d_middle_ref[...] = d_middle
    d_att = (row(vec_ref, "scale_one") * d_middle).astype(bf16)
    d_att_ref[...] = d_att
    d_heads_t_ref[...] = dot_nt(weight_o[...], d_att).astype(bf16)

    def column(values):
        return jnp.sum(values, axis=0, keepdims=True)

    sum_ref[0:1] += column(d_act * unit)
    sum_ref[1:2] += column(d_act)
    sum_ref[2:3] += column(d_middle * attended_ref[...].astype(f32))
    sum_ref[3:4] += column(d_att.astype(f32))


def norm_back(at, numbers, d_hidden, g, middle, attended, vecs, expand_p, out_p):
    tokens, hidden = d_hidden.shape
    width = g.shape[1]
    counts = (len(expand_p), len(out_p))
    block = pl.BlockSpec((SLOTS, width), lambda i, _: (i, 0))
    block_t = pl.BlockSpec((width, SLOTS), lambda i, _: (0, i))
    block_f = pl.BlockSpec((SLOTS, hidden), lambda i, _: (i, 0))
    return pl.pallas_call(
        functools.partial(norm_body, at, counts),
        grid_spec=pltpu.PrefetchScalarGridSpec(
            num_scalar_prefetch=1,
            grid=(tokens // SLOTS,),
            in_specs=[block_f, block, block, block, whole(vecs.shape)]
            + [any_spec] * sum(counts),
            out_specs=[block, block, block_t, whole((8, width))],
            scratch_shapes=[
                pltpu.VMEM((width, hidden), bf16),
                pltpu.VMEM((width, width), bf16),
                pltpu.SemaphoreType.DMA((2, max(counts))),
            ],
        ),
        out_shape=[
            far((tokens, width), f32),
            near((tokens, width), bf16),
            near((width, tokens), bf16),
            jax.ShapeDtypeStruct((8, width), f32),
        ],
        compiler_params=params(32, "arbitrary"),
        cost_estimate=cost(
            2 * tokens * width * hidden + 2 * tokens * width * width, 7 * tokens * hidden
        ),
        name="norm_back",
    )(
        numbers,
        in_vmem(d_hidden),
        in_hbm(g),
        in_vmem(middle),
        in_vmem(attended),
        vecs,
        *map(in_hbm, expand_p + out_p),
    )


def output_body(at, n_pieces, numbers, active_ref, middle_ref, g_ref, vec_ref, *rest):
    pieces = rest[:n_pieces]
    out_ref, sum_ref, weight, sems = rest[n_pieces:]
    step = pl.program_id(0)

    @pl.when(step == 0)
    def _():
        copies = piece_copies(pieces, numbers, weight, sems, at)
        for copy in copies:
            copy.start()
        sum_ref[...] = jnp.zeros_like(sum_ref)
        for copy in copies:
            copy.wait()

    down = dot_nn(active_ref[...], weight[...]) + row(vec_ref, "reduce_bias")
    out_ref[...] = (middle_ref[...] + row(vec_ref, "scale_two") * down).astype(bf16)
    sum_ref[...] += jnp.sum(g_ref[...].astype(f32) * down, axis=0, keepdims=True)


def output(at, numbers, active, middle, g, vecs, pieces):
    tokens, hidden = active.shape
    width = g.shape[1]
    block = pl.BlockSpec((SLOTS, width), lambda i, _: (i, 0))
    return pl.pallas_call(
        functools.partial(output_body, at, len(pieces)),
        grid_spec=pltpu.PrefetchScalarGridSpec(
            num_scalar_prefetch=1,
            grid=(tokens // SLOTS,),
            in_specs=[
                pl.BlockSpec((SLOTS, hidden), lambda i, _: (i, 0)),
                block,
                block,
                whole(vecs.shape),
            ]
            + [any_spec] * len(pieces),
            out_specs=[block, whole((1, width))],
            scratch_shapes=[
                pltpu.VMEM((hidden, width), bf16),
                pltpu.SemaphoreType.DMA((len(pieces),)),
            ],
        ),
        out_shape=[
            far((tokens, width), bf16),
            jax.ShapeDtypeStruct((1, width), f32),
        ],
        compiler_params=params(28, "arbitrary"),
        cost_estimate=cost(2 * tokens * width * hidden, 3 * tokens * hidden),
        name="output",
    )(numbers, in_hbm(active), in_vmem(middle), in_hbm(g), vecs, *map(in_hbm, pieces))


def attend_back_body(
    first,
    count,
    sizes,
    d_heads_t_ref,
    value_ref,
    q_t_ref,
    k_t_ref,
    exp_ref,
    inv_ref,
    d_mixed_ref,
    tile_ref,
    token_ref,
    d_probs,
    d_scores,
    d_outs,
    columns,
):
    image = pl.program_id(0)

    @pl.when(image == 0)
    def _():
        tile_ref[...] = jnp.zeros_like(tile_ref)

    token_ref[...] = jnp.zeros_like(token_ref)
    by_slot, by_spot = place_pair([sizes[SIZES + 3 * image + k] for k in range(3)], 0)
    for k in range(count):
        pair = slice(k // 2 * 2 * HEAD, (k // 2 + 1) * 2 * HEAD)
        d_out = d_heads_t_ref[k * HEAD : (k + 1) * HEAD, :]
        d_probs[k] = dot_nn(value_ref[:, pair], in_pair(d_out, k))
    for k in range(count):
        low, high = k * HEAD, (k + 1) * HEAD
        inverse = inv_ref[0, first + k : first + k + 1, :]
        wide = exp_ref[0, k].astype(f32)
        prob_grad = d_probs[k]
        inner = jnp.sum(prob_grad * wide, axis=0, keepdims=True) * inverse
        d_scores[k] = ((prob_grad - inner) * inverse * wide).astype(bf16)
        d_outs[low:high, :] = (d_heads_t_ref[low:high, :].astype(f32) * inverse).astype(bf16)
    base = count * HEAD
    for k in range(count):
        low, high = k * HEAD, (k + 1) * HEAD
        d_query = dot_nn(k_t_ref[low:high, :], d_scores[k])
        d_mixed_ref[low:high, :] = (d_query.astype(bf16) * 0.125).astype(bf16)
        d_keys = dot_nt(q_t_ref[low:high, :], d_scores[k])
        d_mixed_ref[base + low : base + high, :] = d_keys.astype(bf16)
        d_values = dot_nt(d_outs[low:high, :], exp_ref[0, k])
        d_mixed_ref[2 * base + low : 2 * base + high, :] = d_values.astype(bf16)
    columns[...] = (
        dot_nn(d_scores[...].reshape(count * SLOTS, SLOTS), by_slot)
        .astype(bf16)
        .reshape(count, SLOTS, SLOTS)
    )
    for k in range(count):
        tile_ref[k] += dot_nn(by_spot, columns[k])


def attend_back(first, count, sizes, d_heads_t, value, q_t, k_t, exponent, inverse):
    width, tokens = d_heads_t.shape
    images = tokens // SLOTS
    heads = inverse.shape[1]
    part = count * HEAD
    at = first // count
    block_t = pl.BlockSpec((part, SLOTS), lambda i, _: (at, i))
    return pl.pallas_call(
        functools.partial(attend_back_body, first, count),
        grid_spec=pltpu.PrefetchScalarGridSpec(
            num_scalar_prefetch=1,
            grid=(images,),
            in_specs=[
                block_t,
                pl.BlockSpec((SLOTS, part), lambda i, _: (i, at)),
                block_t,
                block_t,
                pl.BlockSpec((1, count, SLOTS, SLOTS), lambda i, _: (i, at, 0, 0)),
                pl.BlockSpec((1, heads, SLOTS), lambda i, _: (i, 0, 0)),
            ],
            out_specs=[
                pl.BlockSpec((3 * part, SLOTS), lambda i, _: (0, i)),
                whole((count, SLOTS, SLOTS)),
                whole(TOKEN),
            ],
            scratch_shapes=[
                pltpu.VMEM((count, SLOTS, SLOTS), f32),
                pltpu.VMEM((count, SLOTS, SLOTS), bf16),
                pltpu.VMEM((part, SLOTS), bf16),
                pltpu.VMEM((count, SLOTS, SLOTS), bf16),
            ],
        ),
        out_shape=[
            near((3 * part, tokens), bf16),
            near((count, SLOTS, SLOTS), f32),
            jax.ShapeDtypeStruct(TOKEN, f32),
        ],
        compiler_params=params(24, "arbitrary"),
        cost_estimate=cost(images * count * 14 * SLOTS**3, 12 * tokens * part),
        name="attend_back",
    )(
        sizes, in_vmem(d_heads_t), *[in_hbm(v) for v in (value, q_t, k_t, exponent, inverse)]
    )


def input_body(at, groups, offsets, x_ref, d_middle_ref, vec_ref, *rest):
    d_mixed_refs = rest[: len(groups)]
    rest = rest[len(groups) :]
    pieces = rest[:-5]
    grad_ref, sum_ref, bias_ref, weight, sems = rest[-5:]
    step = pl.program_id(0)
    width = x_ref.shape[1]

    @pl.when(step == 0)
    def _():
        copies = piece_copies(pieces, offsets, weight, sems, at)
        for copy in copies:
            copy.start()
        sum_ref[...] = jnp.zeros_like(sum_ref)
        bias_ref[...] = jnp.zeros_like(bias_ref)
        for copy in copies:
            copy.wait()

    total = None
    ones = jnp.ones((16, SLOTS), bf16)
    for (first, count), ref in zip(groups, d_mixed_refs, strict=True):
        part = count * HEAD
        for k in range(3):
            column = k * width + first * HEAD
            block = ref[k * part : (k + 1) * part, :]
            term = dot_nn(weight[:, column : column + part], block)
            total = term if total is None else total + term
            if k != 1:
                line = k // 2
                bias_ref[line : line + 1, first * HEAD : first * HEAD + part] += dot_nt(
                    ones, block
                )[:1]
    d_act = total.T
    unit, inverse = normal_stats(x_ref[...].astype(f32))
    sum_ref[0:1] += jnp.sum(d_act * unit, axis=0, keepdims=True)
    sum_ref[1:2] += jnp.sum(d_act, axis=0, keepdims=True)
    scaled = d_act * row(vec_ref, "gain_one")
    grad_ref[...] = (
        d_middle_ref[...]
        + inverse
        * (
            scaled
            - jnp.mean(scaled, axis=-1, keepdims=True)
            - unit * jnp.mean(scaled * unit, axis=-1, keepdims=True)
        )
    ).astype(bf16)


def input_back(at, offsets, x, d_middle, vecs, groups, d_mixed, pieces):
    tokens, width = x.shape
    block = pl.BlockSpec((SLOTS, width), lambda i, _: (i, 0))
    return pl.pallas_call(
        functools.partial(input_body, at, groups),
        grid_spec=pltpu.PrefetchScalarGridSpec(
            num_scalar_prefetch=1,
            grid=(tokens // SLOTS,),
            in_specs=[block, block, whole(vecs.shape)]
            + [pl.BlockSpec((m.shape[0], SLOTS), lambda i, _: (0, i)) for m in d_mixed]
            + [any_spec] * len(pieces),
            out_specs=[block, whole((8, width)), whole((8, width))],
            scratch_shapes=[
                pltpu.VMEM((width, 3 * width), bf16),
                pltpu.SemaphoreType.DMA((len(pieces),)),
            ],
        ),
        out_shape=[
            far((tokens, width), bf16),
            jax.ShapeDtypeStruct((8, width), f32),
            jax.ShapeDtypeStruct((8, width), f32),
        ],
        compiler_params=params(28, "arbitrary"),
        cost_estimate=cost(6 * tokens * width * width, 14 * tokens * width),
        name="input_back",
    )(offsets, in_hbm(x), in_hbm(d_middle), vecs, *map(in_vmem, d_mixed), *map(in_hbm, pieces))


def rows_body(steps, forms, numbers, *refs):
    n = len(steps)
    lefts, rights = refs[:n], refs[n : 2 * n]
    keep_ref, send_ref, token_ref, gathered, sems = refs[2 * n :]
    token_ref[...] = jnp.zeros_like(token_ref)
    step = pl.program_id(0)
    share = keep_ref.shape[1]

    @pl.when(step == 0)
    def _():
        copies = [
            pltpu.make_async_copy(
                left.at[pl.ds(pl.multiple_of(numbers[KEPT + b] * share, 16), share)],
                gathered.at[which, pl.ds(b * share, share)],
                sems.at[which, b],
            )
            for which, left in enumerate(lefts)
            for b in range(2 * CHIPS)
        ]
        for copy in copies:
            copy.start()
        for copy in copies:
            copy.wait()

    start = 0
    for which in range(n):

        @pl.when((step >= start) & (step < start + steps[which]))
        def _():
            dot = dot_nt if forms[which] else dot_nn
            grad = dot(gathered[which], rights[which][...]).astype(bf16)
            for b in range(CHIPS):
                keep_ref[b] = grad[b * share : (b + 1) * share]
                send_ref[b] = grad[(CHIPS + b) * share : (CHIPS + b + 1) * share]

        start += steps[which]


def grad_rows(numbers, lefts, rights, forms, column):
    width, tokens = lefts[0].shape
    share = width // (2 * CHIPS)
    steps = [right.shape[0 if form else 1] // column for right, form in zip(rights, forms)]
    in_specs = [any_spec] * len(lefts)
    start = 0
    for form, many in zip(forms, steps, strict=True):

        def index(i, _, start=start, many=many, form=form):
            at = jnp.clip(i - start, 0, many - 1)
            return (at, 0) if form else (0, at)

        in_specs.append(pl.BlockSpec((column, tokens) if form else (tokens, column), index))
        start += many
    grad = pl.BlockSpec((CHIPS, share, column), lambda i, _: (0, 0, i))
    return pl.pallas_call(
        functools.partial(rows_body, steps, forms),
        grid_spec=pltpu.PrefetchScalarGridSpec(
            num_scalar_prefetch=1,
            grid=(start,),
            in_specs=in_specs,
            out_specs=[grad, grad, whole(TOKEN)],
            scratch_shapes=[
                pltpu.VMEM((len(lefts), width, tokens), bf16),
                pltpu.SemaphoreType.DMA((len(lefts), 2 * CHIPS)),
            ],
        ),
        out_shape=[far((CHIPS, share, start * column), bf16)] * 2
        + [jax.ShapeDtypeStruct(TOKEN, f32)],
        compiler_params=params(28, "arbitrary"),
        cost_estimate=cost(2 * tokens * width * start * column, 2 * tokens * start * column),
        name="grad_rows",
    )(numbers, *map(in_hbm, lefts), *map(in_vmem, rights))


def swap(values, bit):
    return lax.ppermute(values, "fsdp", [(k, k ^ bit) for k in range(FAST_GROUP)])


BITS = (0, 2, 4, 6, 1, 3, 5, 7)


def gather_near(shard):
    return [shard] + [swap(shard, bit) for bit in (2, 4, 6)]


def gather_rest(pieces):
    return pieces + [swap(piece, 1) for piece in pieces]


def piece_rows(me, rows):
    return [(me ^ bit) * rows for bit in BITS]


def step_rows(me, rows):
    return [((bit >> 1) * 2 + ((me ^ bit) & 1)) * rows for bit in BITS]


def add_all(*terms):
    total = terms[0].astype(f32)
    for term in terms[1:]:
        total = total + term.astype(f32)
    return total.astype(bf16)


def after(value, *others):
    return lax.optimization_barrier((value, others))[0]


def leaves(values):
    return jax.tree.leaves(values)


def gate(values, *tokens):
    values = list(values)

    def body(*refs):
        pass

    out = pl.pallas_call(
        body,
        in_specs=[any_spec] * (len(values) + len(tokens)),
        out_specs=[any_spec] * len(values),
        out_shape=[jax.ShapeDtypeStruct(value.shape, value.dtype) for value in values],
        input_output_aliases={k: k for k in range(len(values))},
        name="gate",
    )(*values, *tokens)
    return list(out)


def trade(block, distance, count):
    return lax.ppermute(block, "rep", [(k, k ^ distance) for k in range(count)])


def scatter_flow(keep, send, rep_count, split, late):
    half = keep.shape[1] // 2
    a, b = slice(0, half), slice(half, None)
    other = swap(send, 1)
    gate = yield [send]
    other = after(other, gate)
    if split:
        x_send = add_all(keep[1::2, a], other[1::2, a])
        y_send = add_all(keep[2:, b], other[2:, b])
        x_got, y_got = swap(x_send, 2), swap(y_send, 4)
        gate = yield [x_send, y_send]
        x_got, y_got = after((x_got, y_got), gate)
        y_next = add_all(keep[2, a], other[2, a], x_got[1])
        x_next = add_all(keep[1, b], other[1, b], y_got[1])
        y_last, x_last = swap(y_next, 4), swap(x_next, 2)
        gate = yield [y_next, x_next]
        y_last, x_last = after((y_last, x_last), gate)
        top = add_all(keep[0, a], other[0, a], x_got[0], y_last)
        bottom = add_all(keep[0, b], other[0, b], y_got[0], x_last)
        own = None
    else:
        sent = [add_all(keep[k], other[k]) for k in (1, 2, 3)]
        got = [swap(block, bit) for block, bit in zip(sent, (2, 4, 6))]
        gate = yield sent
        got = after(got, gate)
        own = add_all(keep[0], other[0], *got)
        top, bottom = own[:half], own[half:]
    if rep_count != 4 or not late:
        if own is None:
            own = jnp.concatenate([top, bottom])
        yield [own]
        return lax.psum(own, "rep")
    me = lax.axis_index("rep")
    low, high = me & 1, me >> 1

    def cut(block, at):
        size = block.shape[0] // 2
        return lax.dynamic_slice_in_dim(block, at * size, size, axis=0)

    given = jnp.where(low == 0, bottom, top)
    got = trade(given, 1, rep_count)
    gate = yield [given]
    got = after(got, gate)
    mine = add_all(jnp.where(low == 0, top, bottom), got)
    given = cut(mine, 1 - high)
    got = trade(given, 2, rep_count)
    gate = yield [given]
    got = after(got, gate)
    own = add_all(cut(mine, high), got)
    got = trade(own, 2, rep_count)
    gate = yield [own]
    got = after(got, gate)
    pair = jnp.where(high == 0, jnp.concatenate([own, got]), jnp.concatenate([got, own]))
    far = trade(pair, 1, rep_count)
    gate = yield [pair]
    far = after(far, gate)
    return jnp.where(
        low == 0, jnp.concatenate([pair, far]), jnp.concatenate([far, pair])
    ).astype(f32)


def small_flow(blocks, me, rep_count):
    shape = blocks.shape[1:]
    blocks = blocks.reshape((2, 2, 2) + shape)
    for axis, bit in enumerate((4, 2, 1)):
        blocks = jnp.where((me & bit) != 0, jnp.flip(blocks, axis), blocks)
    blocks = blocks.reshape((4, 2) + shape)
    keep, send = blocks[:, 0], blocks[:, 1]
    for bit in (1, 2, 4):
        got = swap(send, bit)
        gate = yield [send]
        total = keep + after(got, gate)
        if bit == 1:
            total = total.reshape((2, 2) + shape)
            keep, send = total[:, 0], total[:, 1]
        elif bit == 2:
            keep, send = total[0], total[1]
    distance = 1
    while distance < rep_count:
        got = trade(total, distance, rep_count)
        gate = yield [total]
        total = total + after(got, gate)
        distance *= 2
    return total


class Flows:
    def __init__(self):
        self.live = {}
        self.done = {}

    def add(self, name, flow):
        next(flow)
        self.live[name] = flow

    def step(self, gate, names):
        out = [gate]
        for name in names.split():
            if name in self.live:
                try:
                    out += self.live[name].send(gate)
                except StopIteration as end:
                    self.done[name] = end.value
                    del self.live[name]
        return out


HEAD_GROUPS = ((0, 8), (8, 4))


def shards(
    rep_count,
    tokens_in,
    image_sizes,
    gain_one,
    shift_one,
    project_in,
    query_bias,
    value_bias,
    bias_table,
    project_out,
    out_bias,
    scale_one,
    gain_two,
    shift_two,
    expand_weight,
    expand_bias,
    reduce_weight,
    reduce_bias,
    scale_two,
    cotangent,
):
    batches, images, slots, width = tokens_in.shape
    tokens = batches * images * slots
    heads = bias_table.shape[1]
    share = gain_one.shape[0]
    group = width // share
    fast = group == FAST_GROUP
    me = lax.axis_index("fsdp") if fast else 0
    x = tokens_in.reshape(tokens, width)
    g = cotangent.reshape(tokens, width)
    sizes = image_sizes.reshape(batches * images, 2)
    counts = 1 + sizes[:, 0] * sizes[:, 1]
    sizes = jnp.stack([counts, sizes[:, 1], (65535 + sizes[:, 1]) // sizes[:, 1]], axis=1)
    sizes = sizes.reshape(-1).astype(jnp.int32)

    vectors = [gain_one, shift_one, query_bias, value_bias, out_bias, scale_one]
    vectors += [gain_two, shift_two, reduce_bias, scale_two]
    count = len(vectors)
    first_weight = jnp.concatenate([project_in, project_out], axis=1)
    weights = (first_weight, expand_weight, reduce_weight)
    order = [(me >> 1) ^ k for k in range(CHIPS)] + [me & 1]
    order += [me ^ 2 * k for k in range(CHIPS)] + [me ^ 2 * k ^ 1 for k in range(CHIPS)]
    vecs, expand_row, flat, got = gather_small(vectors, expand_bias, bias_table, group)
    if fast:
        in_p = gather_near(after(first_weight, got))
        rows = [piece_rows(me, weight.shape[0]) for weight in weights]
        rows.append(step_rows(me, reduce_weight.shape[0]))
        groups = [bit >> 1 for bit in BITS]
    else:
        in_p, expand_p, reduce_p = [
            [lax.all_gather(weight, "fsdp", axis=0, tiled=True)] for weight in weights
        ]
        rows = [[0]] * 4
        groups = [0]
    pieces = len(rows[0])
    in_at, expand_at, reduce_at, steps_at = [
        SIZES + sizes.shape[0] + k * pieces for k in range(4)
    ]
    listed = [jnp.asarray(value, jnp.int32) for value in sum(rows, [])]
    numbers = [jnp.asarray(value, jnp.int32) for value in order]
    numbers = jnp.concatenate([jnp.stack(numbers), sizes, jnp.stack(listed)])

    flows = Flows()

    def scatter(name, keep, send, split, late):
        if fast:
            flows.add(name, scatter_flow(keep, send, rep_count, split, late))
        else:
            both = jnp.stack([keep, send], axis=1).reshape(-1, keep.shape[2])
            both = lax.psum_scatter(both, "fsdp", scatter_dimension=0, tiled=True)
            flows.done[name] = lax.psum(both, "rep").astype(f32)

    act_one, act_one_t, d_down, grad_reduce_add = prepare(x, g, vecs)
    tiles, tiles_token = build_tiles(flat, heads)
    if fast:
        in_p = in_p[:1] + gate(in_p[1:], tiles_token, grad_reduce_add)
        in_p = gather_rest(in_p)
        expand_p = gather_near(after(expand_weight, in_p))
    value, q_t, k_t, exponent, inverse, heads_t, heads_out = attend(
        in_at, numbers, act_one, vecs, tiles, in_p
    )
    if fast:
        expand_p = gather_rest(expand_p[:1] + gate(expand_p[1:], inverse))
        reduce_p = gather_near(after(reduce_weight, expand_p))
    attended, middle, act_two, act_two_t, token = project(
        in_at, numbers, heads_out, x, vecs, in_p
    )
    active, slope, reduce_keep, reduce_send, token = expand(
        expand_at, numbers, act_two, d_down, expand_row, expand_p
    )
    if fast:
        reduce_p = gather_rest(reduce_p[:1] + gate(reduce_p[1:], token))
    scatter("reduce", reduce_keep, reduce_send, False, False)
    d_hidden, expand_sum, expand_keep, expand_send = hidden_back(
        steps_at, numbers, d_down, slope, act_two_t, reduce_p, groups
    )
    sent = flows.step(expand_sum, "reduce")
    scatter("expand", expand_keep, expand_send, True, True)
    d_middle, d_att, d_heads_t, sums_two = norm_back(
        (expand_at, in_at), after(numbers, sent), d_hidden, g, middle, attended, vecs, expand_p, in_p
    )
    sent = flows.step(sums_two, "expand")
    (first_a, many_a), (first_b, many_b) = HEAD_GROUPS
    shared = (value, q_t, k_t, exponent, inverse)
    mixed_a, tiles_a, token = attend_back(
        first_a, many_a, after(numbers, sent), d_heads_t, *shared
    )
    sent = flows.step(token, "reduce")
    in_keep_a, in_send_a, token = grad_rows(
        after(numbers, sent), [act_one_t, heads_t], [mixed_a, d_att], [True, False], 768
    )
    sent = flows.step(token, "reduce expand")
    scatter("in_a", in_keep_a, in_send_a, True, True)
    mixed_b, tiles_b, token = attend_back(
        first_b, many_b, after(numbers, sent), d_heads_t, *shared
    )
    sent = flows.step(token, "in_a")
    in_keep_b, in_send_b, token = grad_rows(
        after(numbers, sent), [act_one_t], [mixed_b], [True], 768
    )
    scatter("in_b", in_keep_b, in_send_b, False, True)
    sent = flows.step(token, "expand")
    table_flat = table_grad(after(numbers, sent), tiles_a, tiles_b)
    sent = flows.step(table_flat, "in_b in_a")
    input_grad, sums_one, sums_mixed = input_back(
        in_at, after(numbers, sent), x, d_middle, vecs, HEAD_GROUPS, [mixed_a, mixed_b], in_p
    )
    sent = flows.step(sums_one, "expand in_a in_b")
    block_out, sums_out = output(
        reduce_at, after(numbers, sent), active, middle, g, vecs, reduce_p
    )
    small_grads = pack_sums(
        group,
        share,
        expand_bias.shape[0],
        bias_table.shape[0],
        sums_one,
        sums_mixed,
        sums_two,
        grad_reduce_add,
        sums_out,
        expand_sum,
        table_flat,
    )
    if fast:
        flows.add("small", small_flow(small_grads, me, rep_count))
        sent = [small_grads]
        while flows.live:
            sent = flows.step(sent, "small expand in_a in_b")
        own = flows.done["small"]
        flows.done["reduce"] = after(flows.done["reduce"], own)
    else:
        own = lax.psum_scatter(small_grads, "fsdp", scatter_dimension=0, tiled=True)
        own = lax.psum(own, "rep")[0]
    grad_reduce, grad_expand, in_a, in_b = [
        flows.done[name].astype(f32) for name in ("reduce", "expand", "in_a", "in_b")
    ]
    parts = []
    for k in range(3):
        for (_, many), grads in zip(HEAD_GROUPS, (in_a, in_b)):
            parts.append(grads[:, k * many * HEAD : (k + 1) * many * HEAD])
    grad_in = jnp.concatenate(parts, axis=1)
    grad_out = in_a[:, 3 * many_a * HEAD :]

    own_vectors = [own[k, :share] for k in range(count)]
    bias_lines = -(-expand_bias.shape[0] // 128)
    own_expand = own[BIAS_ROWS : BIAS_ROWS + bias_lines].reshape(-1)[: expand_bias.shape[0]]
    own_table = own[TABLE_ROWS : TABLE_ROWS + heads, : bias_table.shape[0]].T
    shape = tokens_in.shape
    return (
        block_out.reshape(shape),
        input_grad.reshape(shape),
        own_vectors[0],
        own_vectors[1],
        grad_in,
        own_vectors[2],
        own_vectors[3],
        own_table,
        grad_out,
        own_vectors[4],
        own_vectors[5],
        own_vectors[6],
        own_vectors[7],
        grad_expand,
        own_expand,
        grad_reduce,
        own_vectors[8],
        own_vectors[9],
    )


def solution(mesh):
    by_image = P(None, ("fsdp", "rep"), None, None)
    line = P("fsdp")
    matrix = P("fsdp", None)
    return jax.shard_map(
        functools.partial(shards, mesh.shape["rep"]),
        mesh=mesh,
        in_specs=(
            by_image,
            P(None, ("fsdp", "rep"), None),
            line,
            line,
            matrix,
            line,
            line,
            matrix,
            matrix,
            line,
            line,
            line,
            line,
            matrix,
            line,
            matrix,
            line,
            line,
            by_image,
        ),
        out_specs=(
            by_image,
            by_image,
            line,
            line,
            matrix,
            line,
            line,
            matrix,
            matrix,
            line,
            line,
            line,
            line,
            matrix,
            line,
            matrix,
            line,
            line,
        ),
        check_vma=False,
    )
```
